128 devices in a mesh: wide: 16 (over x_lo, z, core), narrow: 8 (over x_hi, y).
Axes of the slice: x: 4 (x_hi: 2, x_lo: 2; x = x_hi * 2 + x_lo), y: 4, z: 4, core: 2. Of those that a mesh axis runs over, the one named last changes fastest.
Arguments:
- residual: bfloat16 [1024, 4096], P(('wide', 'narrow')), may hold values from -6 to 6
- queries: bfloat16 [1024, 8192], P(('wide', 'narrow')), may hold values from -6 to 6
- key_cache: bfloat16 [1024, 256, 512], P(('wide', 'narrow')), may hold values from -6 to 6
- value_cache: bfloat16 [1024, 256, 512], P(('wide', 'narrow')), may hold values from -6 to 6
- new_keys: bfloat16 [1024, 512], P(('wide', 'narrow')), may hold values from -6 to 6
- new_values: bfloat16 [1024, 512], P(('wide', 'narrow')), may hold values from -6 to 6
- lengths: int32 [1024], P(('wide', 'narrow')), may hold values from 2 to 256, as said below
- out_weight: bfloat16 [8192, 4096], P('narrow'), may hold values from -0.25 to 0.25
- norm_gain: float32 [4096], replicated, may hold values from 0.25 to 1.75
- routes: int32 [1024, 8], P(('wide', 'narrow')), may hold values from 0 to 63, all different within a row; in each aligned block of 8 rows (0 to 7, 8 to 15, ...) at most 2 rows name the same one
- gate_probs: float32 [1024, 8], P(('wide', 'narrow')), may hold values from 0.02 to 1
- w_gate: bfloat16 [128, 4096, 384], P(('wide', 'narrow')), may hold values from -0.09375 to 0.09375
- w_up: bfloat16 [128, 4096, 384], P(('wide', 'narrow')), may hold values from -0.09375 to 0.09375
- w_down: bfloat16 [128, 384, 4096], P(('wide', 'narrow')), may hold values from -0.21875 to 0.21875
Outputs:
- mixed: bfloat16 [1024, 4096], P(('wide', 'narrow'))
The draws below stay inside these ranges and needn't reach their ends.
Inputs may be any that keep to these rules, and one draw needn't show every extreme that they name: `lengths`: some request holds exactly 256 cached positions. `routes`: in the rows of one device (aligned blocks of 8 rows) no expert is named by more than 2 rows; some expert is named by exactly 2.
All inputs are finite; a program needn't handle non-finite values.
Results may differ from the reference program's by a relative error of at most 0.017.
Values may be sent and summed in bfloat16 or wider, within the bound.
A program may use at most 128 MiB of HBM per device.

```python
import math
import jax
import jax.numpy as jnp
import numpy as np
from jax import lax

D = 4096
HQ = 64
KVH = 4
HD = 128
EH = 768
TOP = 8
REQ_DEV = 8
CACHE = 256
REQUESTS = 1024
EXPERTS = 64
CAP = 2


def draw_queries(key, part):
    key = jax.random.fold_in(key, 1)
    drawn = jnp.clip(jax.random.normal(key, (REQUESTS, HQ * HD), jnp.float32), -6.0, 6.0)
    return drawn.astype(jnp.bfloat16)


def draw_key_cache(key, part):
    key = jax.random.fold_in(key, 2)
    drawn = jnp.clip(jax.random.normal(key, (REQUESTS, CACHE, KVH * HD), jnp.float32), -6.0, 6.0)
    return drawn.astype(jnp.bfloat16)


def draw_lengths(key, part):
    key = jax.random.fold_in(key, 3)
    drawn = jax.random.randint(key, (REQUESTS,), 2, CACHE + 1, dtype=jnp.int32)
    longest = jax.random.randint(jax.random.fold_in(key, 1), (), 0, REQUESTS, dtype=jnp.int32)
    return drawn.at[longest].set(CACHE)


def block_scale(own_key, shape, cuts, smallest, high):
    loudness = 1.0
    for position, blocks in cuts:
        heights = jax.random.uniform(jax.random.fold_in(jax.random.fold_in(own_key, 6), position), (blocks,), jnp.float32, smallest / len(cuts), high / len(cuts))
        loudness = loudness * jnp.repeat(jnp.exp(heights), shape[position] // blocks).reshape((-1,) + (1,) * (len(shape) - 1 - position))
    return loudness


def assign_block(key, own, number, rows, count, top, reach, skew):
    order = jax.random.permutation(key, count)
    heavy_load, usual = portions_of(count, rows * top, reach, skew, True), portions_of(count, rows * top, reach, skew, False)
    places = jnp.arange(count)

    def named(sizes, turn):
        used = int((sizes > 0).sum())
        fixed = max(1, used // 4)
        shifted = fixed + (places - fixed + turn * (used - fixed)) % max(1, count - fixed)
        return jnp.zeros((count,), jnp.int32).at[order[jnp.where(places < fixed, places, shifted)]].set(jnp.asarray(sizes, jnp.int32))

    sizes = jnp.where(number % 4 == 0, named(heavy_load, number // 4), named(usual, number - number // 4 - 1))
    mixed = jax.random.permutation(jax.random.fold_in(own, 3), count)
    donor, receiver = mixed[0:count // 2 * 2:2], mixed[1:count // 2 * 2:2]
    slack = jnp.minimum(sizes[donor] - 1, reach - sizes[receiver]) // 2
    slack = jnp.where((donor == order[0]) | (receiver == order[0]) | (sizes[receiver] == 0), 0, jnp.maximum(slack, 0))
    shifted = jax.random.randint(jax.random.fold_in(own, 4), (count // 2,), 0, 1 << 20) % (slack + 1)
    sizes = sizes.at[donor].add(-shifted).at[receiver].add(shifted)
    labels = jnp.searchsorted(jnp.cumsum(sizes), jnp.arange(rows * top), side="right").astype(jnp.int32)
    listing = labels.reshape(top, rows).T
    listing = listing[jax.random.permutation(jax.random.fold_in(own, 1), rows)]
    turn = jax.random.randint(jax.random.fold_in(own, 2), (rows, 1), 0, top)
    return jnp.take_along_axis(listing, (jnp.arange(top)[None, :] + turn) % top, axis=1)


def portions_of(count, total, reach, skew, full):
    portions = [(1 << 20) // math.isqrt(grade ** skew) + 1 for grade in range(1, count + 1)]
    largest = reach if full else min(reach, max(-(-total // count), total * portions[0] // sum(portions)))
    least = 1 if total - largest >= count - 1 else 0
    holding, spare = [largest] + [least] * (count - 1), total - largest - least * (count - 1)
    while spare > 0:
        movable = [i for i in range(1, count) if holding[i] < largest] or [i for i in range(1, count) if holding[i] < reach]
        mass, budget = sum([portions[i] for i in movable]), spare
        for i in movable:
            extra = min(reach - holding[i], max(1, budget * portions[i] // mass), spare)
            holding[i] = holding[i] + extra
            spare = spare - extra
    return np.array(holding)


def noise(key, extent, width, limit, cuts=(), kind=jnp.bfloat16):
    loudness = block_scale(key, extent, cuts, -0.22, 0.18) if cuts else 1.0
    entries = jax.random.normal(key, extent, jnp.float32) * width * loudness
    return jnp.minimum(jnp.maximum(entries, -limit), limit).astype(kind)


def setup_inputs(seed: int = 0) -> dict:
    keys = jax.random.split(jax.random.key(seed), 15)
    residual = noise(keys[0], (REQUESTS, D), 1.0, 6.0, ((0, 128),))
    queries = draw_queries(jax.random.fold_in(keys[14], 71), 0)
    key_cache = draw_key_cache(jax.random.fold_in(keys[14], 71), 0)
    value_cache = noise(keys[3], (REQUESTS, CACHE, KVH * HD), 1.0, 6.0, ((0, 128),))
    new_keys = noise(keys[4], (REQUESTS, KVH * HD), 1.0, 6.0, ((0, 128),))
    new_values = noise(keys[5], (REQUESTS, KVH * HD), 1.0, 6.0, ((0, 128),))
    lengths = draw_lengths(jax.random.fold_in(keys[14], 71), 0)
    out_weight = noise(keys[7], (HQ * HD, D), (HD * 4) ** -0.5, 0.25, ((0, 8),))
    norm_gain = jnp.clip(1.0 + 0.15 * jax.random.normal(keys[8], (D,), jnp.float32), 0.25, 1.75)
    routes_keys = jax.random.split(jax.random.fold_in(keys[9], 1), REQUESTS // REQ_DEV)
    routes_turns = jax.random.permutation(jax.random.fold_in(keys[9], 3), REQUESTS // REQ_DEV)
    routes = jax.vmap(lambda own, number: assign_block(jax.random.fold_in(keys[9], 2), own, number, REQ_DEV, EXPERTS, TOP, CAP, 2))(routes_keys, routes_turns).reshape((REQUESTS, TOP))
    gate_probs = jnp.clip(jnp.exp(math.log(1.0) - 3.912023 * jax.random.uniform(keys[10], (REQUESTS, TOP), jnp.float32) ** block_scale(keys[10], (REQUESTS, TOP), ((0, 128),), -0.2, 0.2)), 0.02, 1.0)
    w_gate = noise(keys[11], (2 * EXPERTS, D, EH // 2), D ** -0.5, 0.09375, ((0, 128),))
    w_up = noise(keys[12], (2 * EXPERTS, D, EH // 2), D ** -0.5, 0.09375, ((0, 128),))
    w_down = noise(keys[13], (2 * EXPERTS, EH // 2, D), EH ** -0.5, 0.21875, ((0, 128),))
    return dict(residual=residual, queries=queries, key_cache=key_cache, value_cache=value_cache, new_keys=new_keys, new_values=new_values, lengths=lengths, out_weight=out_weight, norm_gain=norm_gain, routes=routes, gate_probs=gate_probs, w_gate=w_gate, w_up=w_up, w_down=w_down)


def attend_block(pieces):
    queries, cached_keys, cached_values, fresh_keys, fresh_values, length = pieces
    batch_rows = queries.shape[0]
    scaling = HD ** (-0.5)
    grouped = queries.astype(jnp.float32).reshape(batch_rows, KVH, HQ // KVH, HD)
    key_heads = cached_keys.astype(jnp.float32).reshape(batch_rows, CACHE, KVH, HD)
    value_heads = cached_values.astype(jnp.float32).reshape(batch_rows, CACHE, KVH, HD)
    scores = jnp.einsum('rgqd,rlgd->rgql', grouped, key_heads) * scaling
    own_score = jnp.einsum('rgqd,rgd->rgq', grouped, fresh_keys.astype(jnp.float32).reshape(batch_rows, KVH, HD)) * scaling
    visible = jnp.arange(CACHE, dtype=jnp.int32)[None, :] < length[:, None]
    scores = jnp.where(visible[:, None, None, :], scores, -jnp.inf)
    highest = jnp.maximum(lax.optimization_barrier(jnp.max(scores, axis=-1)), own_score)
    weights = jnp.exp(scores - highest[..., None])
    own_weight = jnp.exp(own_score - highest)
    normaliser = lax.optimization_barrier(jnp.sum(weights, axis=-1)) + own_weight
    weights = (weights / normaliser[..., None]).astype(jnp.bfloat16)
    own_weight = (own_weight / normaliser).astype(jnp.bfloat16)
    attended = jnp.einsum('rgql,rlgd->rgqd', weights.astype(jnp.float32), value_heads)
    attended = attended + own_weight.astype(jnp.float32)[..., None] * fresh_values.astype(jnp.float32).reshape(batch_rows, KVH, 1, HD)
    return attended.reshape(batch_rows, HQ * HD).astype(jnp.bfloat16)

def expert_rows(token_rows, gate_pair, up_pair, down_pair):
    summed = jnp.zeros((token_rows.shape[0], D), jnp.float32)
    for portion in range(2):
        gate_value = jnp.dot(token_rows, gate_pair[portion], preferred_element_type=jnp.float32)
        up_value = jnp.dot(token_rows, up_pair[portion], preferred_element_type=jnp.float32)
        active = (jax.nn.silu(gate_value) * up_value).astype(jnp.bfloat16)
        summed = summed + jnp.dot(active, down_pair[portion], preferred_element_type=jnp.float32)
    return summed.astype(jnp.bfloat16)

def reference(residual, queries, key_cache, value_cache, new_keys, new_values, lengths, out_weight, norm_gain, routes, gate_probs, w_gate, w_up, w_down):
    sources = REQUESTS // REQ_DEV

    def split_rows(array):
        return array.reshape((sources, REQ_DEV) + array.shape[1:])
    attended = lax.map(attend_block, tuple((split_rows(item) for item in (queries, key_cache, value_cache, new_keys, new_values, lengths))))
    attended = attended.reshape(REQUESTS, HQ * HD)
    attention_sum = jnp.dot(attended, out_weight, preferred_element_type=jnp.float32)
    stream = (residual.astype(jnp.float32) + attention_sum).astype(jnp.bfloat16)
    stream_float = stream.astype(jnp.float32)
    mean_square = lax.optimization_barrier(jnp.mean(stream_float * stream_float, axis=-1, keepdims=True))
    normed = (stream_float * lax.rsqrt(mean_square + 1e-06) * norm_gain).astype(jnp.bfloat16)
    chosen = routes.reshape(sources, REQ_DEV * TOP)
    onehot = (chosen[..., None] == jnp.arange(EXPERTS, dtype=jnp.int32)).astype(jnp.int32)
    earlier = jnp.cumsum(onehot, axis=1) - onehot
    slot_index = lax.optimization_barrier(jnp.sum(onehot * earlier, axis=-1))
    source_ids = jnp.arange(sources, dtype=jnp.int32)[:, None]
    target = chosen * (sources * CAP) + source_ids * CAP + slot_index
    row_index = source_ids * REQ_DEV + jnp.arange(REQ_DEV * TOP, dtype=jnp.int32)[None, :] // TOP
    table = jnp.zeros((EXPERTS * sources * CAP,), jnp.int32).at[target.reshape(-1)].set(row_index.reshape(-1))

    def per_expert(pieces):
        selection, gate_pair, up_pair, down_pair = pieces
        return expert_rows(normed[selection], gate_pair, up_pair, down_pair)
    outputs = lax.map(per_expert, (table.reshape(EXPERTS, sources * CAP), w_gate.reshape(EXPERTS, 2, D, EH // 2), w_up.reshape(EXPERTS, 2, D, EH // 2), w_down.reshape(EXPERTS, 2, EH // 2, D)))
    outputs = outputs.reshape(EXPERTS * sources * CAP, D)
    picked = outputs[target.reshape(-1)].astype(jnp.float32).reshape(REQUESTS, TOP, D)
    shares = gate_probs / lax.optimization_barrier(jnp.sum(gate_probs, axis=-1, keepdims=True))
    expert_mix = lax.optimization_barrier(jnp.sum(shares[..., None] * picked, axis=1))
    return (stream_float + expert_mix).astype(jnp.bfloat16)
```

```python
import functools

import jax
import jax.numpy as jnp
from jax import lax
from jax.experimental import pallas as pl
from jax.experimental.pallas import tpu as pltpu
from jax.sharding import PartitionSpec as P

MESH = pl.DeviceIdType.MESH
F32 = jnp.float32
BF16 = jnp.bfloat16

D = 4096
HALF = 2048
HQ = 64
KVH = 4
HD = 128
TOP = 8
CACHE = 256
ROWS = 8
EH = 384

CW = (640, 640, 768)
OFF = (0, 640, 1280)
ORD = ((0, 1, 2), (1, 2, 0), (2, 0, 1))
STEPS = (1, 3, 2)


def coords():
    w, n = lax.axis_index("wide"), lax.axis_index("narrow")
    c = lax.rem(w, 2)
    z = lax.rem(lax.div(w, 2), 4)
    x = lax.div(n, 4) * 2 + lax.div(w, 8)
    return (x, lax.rem(n, 4), z), c, w * 8 + n, n


def device(pos, c):
    x, y, z = pos
    return (lax.rem(x, 2) * 8 + z * 2 + c, lax.div(x, 2) * 4 + y)


def shift(pos, axis, d):
    moved = list(pos)
    moved[axis] = lax.rem(moved[axis] + d, 4)
    return tuple(moved)


def remote(src, dst, ssem, rsem, target):
    return pltpu.make_async_remote_copy(
        src_ref=src, dst_ref=dst, send_sem=ssem, recv_sem=rsem, device_id=target, device_id_type=MESH
    )


def line_index(pos, p, stage, q, half=None):
    order = ORD[p]
    idx = list(pos)
    idx[order[stage]] = q
    for s in range(stage):
        idx[order[s]] = slice(None)
    if half is not None:
        idx[order[0]] = pl.ds(2 * half, 2)
    return tuple(idx)


def slab_index(p, first=slice(None), second=slice(None)):
    order = ORD[p]
    spec = {order[0]: first, order[1]: second}
    return tuple(spec[axis] for axis in range(3) if axis != order[2])


def kernel(
    residual, queries, key_cache, value_cache, new_keys, new_values, lengths, out_weight, norm_gain,
    routes, gate_probs, w_gate, w_up, w_down,
    out,
    keys, values, wo, wgu, wd, att, att_rx, a_mat, y_tx, y_rx, res_tx, res_rx, sq_tx, sq_rx,
    share, gh0, gh1, gh2, acc, act, p0, p1, p2, ra0, ra1, ra2, rx0, rx1, rx2, ry0, ry1, ry2,
    rz0, rz1, rz2, kept, fin_tx, fin_rx,
    lsem, pair_s, pair_r, a2a_s, a2a_r, af_s, af_r, y_s, y_r, sh_s, sh_r,
    g1_s, g1_r, g3_s, g3_r, d_s, d_r, act_s, act_r, q3_s, q3_r, q1_s, q1_r,
):
    pos, c, me, n_me = coords()
    x, y, z = pos
    sib = device(pos, 1 - c)
    gh = (gh0, gh1, gh2)
    part = (p0, p1, p2)
    ra, rx, ry, rz = (ra0, ra1, ra2), (rx0, rx1, rx2), (ry0, ry1, ry2), (rz0, rz1, rz2)
    own_cols = pl.ds(pl.multiple_of(c * HALF, HALF), HALF)
    other_cols = pl.ds(pl.multiple_of((1 - c) * HALF, HALF), HALF)
    sends = []

    def send(src, dst, ssem, rsem, target, keep=True):
        copy = remote(src, dst, ssem, rsem, target)
        copy.start()
        if keep:
            sends.append(copy)

    def arrived(dst, ssem, rsem):
        remote(dst, dst, ssem, rsem, sib).wait_recv()

    group = [(dx, dy) for dx in range(2) for dy in range(4)]

    def member(dx, dy):
        gx = x if dx == 0 else 3 - x
        gy = lax.rem(y + dy, 4)
        return (gx, gy, z), lax.div(gx, 2) * 4 + gy

    local = [
        pltpu.make_async_copy(key_cache, keys, lsem.at[0]),
        pltpu.make_async_copy(value_cache, values, lsem.at[1]),
        pltpu.make_async_copy(out_weight.at[:, own_cols], wo, lsem.at[2]),
        pltpu.make_async_copy(w_gate.at[0], wgu.at[:, pl.ds(0, EH)], lsem.at[3]),
        pltpu.make_async_copy(w_up.at[0], wgu.at[:, pl.ds(EH, EH)], lsem.at[4]),
        pltpu.make_async_copy(w_down.at[0, :, own_cols], wd.at[c], lsem.at[5]),
    ]
    for copy in local[:3]:
        copy.start()

    barrier = pltpu.get_barrier_semaphore()
    partners = [sib] + [device(shift(pos, a, d), c) for a in range(3) for d in STEPS]
    partners += [device(member(1, dy)[0], c) for dy in (1, 2, 3)]
    for partner in partners:
        pl.semaphore_signal(barrier, inc=1, device_id=partner, device_id_type=MESH)

    probs = gate_probs[...]
    shares = probs / jnp.sum(probs, axis=-1, keepdims=True)
    lanes = lax.broadcasted_iota(jnp.int32, (ROWS, 128), 1)
    dense = jnp.zeros((ROWS, 128), F32)
    chosen = routes[...]
    for k in range(TOP):
        dense = dense + jnp.where(chosen[:, k : k + 1] == lanes, shares[:, k : k + 1], 0.0)
    share[x, y, z, c] = dense
    res_tx[...] = residual[:, other_cols].astype(F32)

    pl.semaphore_wait(barrier, len(partners))
    send(res_tx, res_rx, pair_s.at[0], pair_r.at[0], sib)
    for k, d in enumerate(STEPS):
        view = share.at[x, y, z, c]
        send(view, view, sh_s.at[0, k], sh_r.at[0, k], device(shift(pos, 0, d), c))

    local[0].wait()
    local[1].wait()
    for copy in local[3:]:
        copy.start()
    send(w_down.at[0, :, other_cols], wd.at[c], pair_s.at[1], pair_r.at[1], sib)
    scaling = HD ** (-0.5)
    row_request = lax.rem(lax.broadcasted_iota(jnp.int32, (128, CACHE), 0), ROWS)
    limit = jnp.zeros((128, CACHE), jnp.int32)
    for r in range(ROWS):
        limit = jnp.where(row_request == r, lengths[r], limit)
    visible = lax.broadcasted_iota(jnp.int32, (128, CACHE), 1) < limit
    for g in range(KVH):
        cols = slice(g * HD, (g + 1) * HD)
        q = jnp.concatenate(
            [queries[:, (g * 16 + h) * HD : (g * 16 + h + 1) * HD].astype(F32) for h in range(16)], axis=0
        )
        scores = lax.dot_general(
            q.astype(BF16), keys[:, :, cols].reshape(ROWS * CACHE, HD), (((1,), (1,)), ((), ())),
            preferred_element_type=F32,
        )
        picked = scores[:, :CACHE]
        for r in range(1, ROWS):
            picked = jnp.where(row_request == r, scores[:, r * CACHE : (r + 1) * CACHE], picked)
        picked = jnp.where(visible, picked * scaling, -jnp.inf)
        fresh = jnp.concatenate([new_keys[:, cols].astype(F32)] * 16, axis=0)
        own = jnp.sum(q * fresh, axis=-1, keepdims=True) * scaling
        highest = jnp.maximum(jnp.max(picked, axis=-1, keepdims=True), own)
        weights = jnp.exp(picked - highest)
        own = jnp.exp(own - highest)
        norm = jnp.sum(weights, axis=-1, keepdims=True) + own
        weights = weights / norm
        own = (own / norm).astype(BF16).astype(F32)
        spread = jnp.concatenate(
            [jnp.where(row_request == r, weights, 0.0).astype(BF16) for r in range(ROWS)], axis=1
        )
        got = jnp.dot(spread, values[:, :, cols].reshape(ROWS * CACHE, HD), preferred_element_type=F32)
        got = got + own * jnp.concatenate([new_values[:, cols].astype(F32)] * 16, axis=0)
        att[2 * g : 2 * g + 2] = got.astype(BF16).reshape(2, 64, HD)

    mine = pltpu.make_async_copy(att.at[n_me], att_rx.at[n_me, c], lsem.at[6])
    mine.start()
    for i, (dx, dy) in enumerate(group):
        if i:
            target, n = member(dx, dy)
            send(att.at[n], att_rx.at[n_me, c], a2a_s.at[i], a2a_r.at[i], device(target, c))
    for k, d in enumerate(STEPS):
        view = share.at[lax.rem(x + 4 - d, 4), y, z, c]
        arrived(view, sh_s.at[0, k], sh_r.at[0, k])
    for k, d in enumerate(STEPS):
        view = share.at[:, y, z, c]
        send(view, view, sh_s.at[1, k], sh_r.at[1, k], device(shift(pos, 1, d), c))
    mine.wait()
    for i, (dx, dy) in enumerate(group):
        _, n = member(dx, (4 - dy) % 4)
        view = att_rx.at[n, c]
        if i:
            arrived(view, a2a_s.at[i], a2a_r.at[i])
        send(view, view, af_s.at[i], af_r.at[i], sib)
    for i, (dx, dy) in enumerate(group):
        _, n = member(dx, (4 - dy) % 4)
        arrived(att_rx.at[n, 1 - c], af_s.at[i], af_r.at[i])

    heads = att_rx[...].astype(F32).reshape(16, 64, HD)
    for h in range(8):
        a_mat[:, h * HD : (h + 1) * HD] = heads[:, h * 8 : (h + 1) * 8].reshape(128, HD).astype(BF16)

    local[2].wait()
    for j in range(4):
        cols = pl.ds(j * 512, 512)
        sums = jnp.dot(a_mat[...], wo[:, cols], preferred_element_type=F32)
        y_tx[:, :, cols] = sums.astype(BF16).reshape(8, 16, 512)
        for i, (dx, dy) in enumerate(group):
            if i:
                target, n = member(dx, dy)
                send(y_tx.at[n, :, cols], y_rx.at[i, :, cols], y_s.at[j, i], y_r.at[j, i], device(target, c))
    for k, d in enumerate(STEPS):
        view = share.at[:, lax.rem(y + 4 - d, 4), z, c]
        arrived(view, sh_s.at[1, k], sh_r.at[1, k])
    for k, d in enumerate(STEPS):
        view = share.at[:, :, z, c]
        send(view, view, sh_s.at[2, k], sh_r.at[2, k], device(shift(pos, 2, d), c))
    acc[...] = jnp.zeros_like(acc)
    arrived(res_rx, pair_s.at[0], pair_r.at[0])
    own_res, other_res = residual[:, own_cols].astype(F32), res_rx[...]
    first = c == 0
    total = jnp.concatenate(
        [jnp.where(first, own_res, other_res), jnp.where(first, other_res, own_res)], axis=0
    )
    attention = y_tx[n_me].astype(F32)
    for i in range(1, 8):
        for j in range(4):
            arrived(y_rx.at[i, :, pl.ds(j * 512, 512)], y_s.at[j, i], y_r.at[j, i])
        attention = attention + y_rx[i].astype(F32)
    stream = (total + attention).astype(BF16).astype(F32)
    squares = jnp.sum(stream * stream, axis=-1, keepdims=True)
    sq_tx[...] = jnp.broadcast_to(squares, (16, 128))
    send(sq_tx, sq_rx, pair_s.at[2], pair_r.at[2], sib)
    kept[...] = stream
    arrived(sq_rx, pair_s.at[2], pair_r.at[2])
    mean = (squares + sq_rx[:, 0:1]) * (1.0 / D)
    normed = (stream * lax.rsqrt(mean + 1e-06) * norm_gain[:, own_cols]).astype(BF16)
    for p in range(3):
        gh[p][(c,) + pos] = normed[:, OFF[p] : OFF[p] + CW[p]]

    def block(p, idx):
        return gh[p].at[(c,) + idx]

    for p in range(3):
        a = ORD[p][0]
        for k, d in enumerate(STEPS):
            view = block(p, pos)
            send(view, view, g1_s.at[p, 0, k], g1_r.at[p, 0, k], device(shift(pos, a, d), c))

    def chunk(p, rel, q):
        order = ORD[p]
        idx = list(line_index(pos, p, 2, q))
        idx[order[1]] = lax.rem(pos[order[1]] + rel, 4)
        return idx

    def send_chunk(p, rel):
        a = ORD[p][2]
        view = block(p, tuple(chunk(p, rel, pos[a])))
        send(view, view, g3_s.at[p, rel, 0], g3_r.at[p, rel, 0], device(shift(pos, a, 1), c))
        send(view, view, g3_s.at[p, rel, 1], g3_r.at[p, rel, 1], device(shift(pos, a, 3), c))

    def half_chunk(p, rel, q, half):
        idx = chunk(p, rel, q)
        idx[ORD[p][0]] = pl.ds(2 * half, 2)
        return block(p, tuple(idx))

    for p in range(3):
        a, b = ORD[p][0], ORD[p][1]
        for k, d in enumerate(STEPS):
            view = block(p, line_index(pos, p, 0, lax.rem(pos[a] + 4 - d, 4)))
            arrived(view, g1_s.at[p, 0, k], g1_r.at[p, 0, k])
        view = block(p, line_index(pos, p, 1, pos[b]))
        for k, d in enumerate(STEPS):
            send(view, view, g1_s.at[p, 1, k], g1_r.at[p, 1, k], device(shift(pos, b, d), c))
        send_chunk(p, 0)
    for k, d in enumerate(STEPS):
        for p in range(3):
            b = ORD[p][1]
            view = block(p, line_index(pos, p, 1, lax.rem(pos[b] + 4 - d, 4)))
            arrived(view, g1_s.at[p, 1, k], g1_r.at[p, 1, k])
            send_chunk(p, 4 - d)

    def pass_on(rel):
        for p in range(3):
            a = ORD[p][2]
            left, right = lax.rem(pos[a] + 3, 4), lax.rem(pos[a] + 1, 4)
            arrived(block(p, tuple(chunk(p, rel, left))), g3_s.at[p, rel, 0], g3_r.at[p, rel, 0])
            view = half_chunk(p, rel, left, 0)
            send(view, view, g3_s.at[p, rel, 2], g3_r.at[p, rel, 2], device(shift(pos, a, 1), c), False)
            arrived(block(p, tuple(chunk(p, rel, right))), g3_s.at[p, rel, 1], g3_r.at[p, rel, 1])
            view = half_chunk(p, rel, right, 1)
            send(view, view, g3_s.at[p, rel, 3], g3_r.at[p, rel, 3], device(shift(pos, a, 3), c), False)

    def slab(p, d):
        a = ORD[p][2]
        return line_index(pos, p, 2, lax.rem(pos[a] + d, 4))

    def to_sibling(d):
        for p in range(3):
            view = block(p, slab(p, d))
            send(view, view, d_s.at[p, d], d_r.at[p, d], sib, False)

    for copy in local[3:]:
        copy.wait()
    to_sibling(0)

    @pl.loop(0, 8)
    def _(i):
        @pl.when(i == 1)
        def _():
            pass_on(0)

        @pl.when(i == 2)
        def _():
            for rel in (3, 1, 2):
                pass_on(rel)
            to_sibling(3)
            to_sibling(1)

        @pl.when(i == 6)
        def _():
            for rel in (0, 3, 1, 2):
                for p in range(3):
                    opposite = lax.rem(pos[ORD[p][2]] + 2, 4)
                    arrived(half_chunk(p, rel, opposite, 0), g3_s.at[p, rel, 2], g3_r.at[p, rel, 2])
                    arrived(half_chunk(p, rel, opposite, 1), g3_s.at[p, rel, 3], g3_r.at[p, rel, 3])
            to_sibling(2)

        s = lax.div(i, 2)
        d = jnp.where(s == 0, 0, jnp.where(s == 1, 3, jnp.where(s == 2, 1, 2)))
        odd = lax.rem(i, 2)
        half = jnp.where(odd == 0, c, 1 - c)

        @pl.when(odd == 1)
        def _():
            for p in range(3):
                arrived(gh[p].at[(1 - c,) + slab(p, d)], d_s.at[p, d], d_r.at[p, d])

        for p in range(3):
            idx = slab(p, d)
            rows = gh[p][(half,) + idx].reshape(256, CW[p])
            k = pl.ds(pl.multiple_of(half * HALF + OFF[p], 128), CW[p])
            sums = jnp.dot(rows, wgu[k, :], preferred_element_type=F32)
            acc[idx] += sums.reshape(4, 4, 16, 2 * EH)

    for k, d in enumerate(STEPS):
        view = share.at[:, :, lax.rem(z + 4 - d, 4), c]
        arrived(view, sh_s.at[2, k], sh_r.at[2, k])
    view = share.at[:, :, :, c]
    send(view, view, pair_s.at[3], pair_r.at[3], sib)
    arrived(share.at[:, :, :, 1 - c], pair_s.at[3], pair_r.at[3])

    expert = lax.div(me, 2)
    wide_lanes = lax.broadcasted_iota(jnp.int32, (64, 128), 1)

    @pl.loop(0, 16)
    def _(i):
        ix, iy = lax.div(i, 4), lax.rem(i, 4)
        weight = jnp.sum(
            jnp.where(wide_lanes == expert, share[ix, iy].reshape(64, 128), 0.0), axis=-1, keepdims=True
        )
        both = acc[ix, iy].reshape(64, 2 * EH)
        gate, up = both[:, :EH], both[:, EH:]
        active = gate / (1.0 + jnp.exp(-gate)) * up * weight
        act[c, ix, iy] = active.astype(BF16).reshape(4, 16, EH)

        @pl.when(iy == 3)
        def _():
            view = act.at[c, ix]
            remote(view, view, act_s.at[ix], act_r.at[ix], sib).start()

    for ix in range(4):
        arrived(act.at[1 - c, ix], act_s.at[ix], act_r.at[ix])
    arrived(wd.at[1 - c], pair_s.at[1], pair_r.at[1])

    halves = (pl.ds(0, 2), pl.ds(2, 2))

    def slab_part(p, d, first=slice(None), second=slice(None)):
        order = ORD[p]
        idx = [None] * 3
        idx[order[0]], idx[order[1]] = first, second
        idx[order[2]] = lax.rem(pos[order[2]] + d, 4)
        return tuple(idx)

    def near(p, stage, d):
        return device(shift(pos, ORD[p][stage], d), c)

    @pl.loop(0, 4)
    def _(s):
        d = jnp.where(s == 0, 2, jnp.where(s == 1, 1, jnp.where(s == 2, 3, 0)))
        for p in range(3):
            idx = slab(p, d)
            cols = pl.ds(OFF[p], CW[p])
            sums = jnp.dot(act[(0,) + idx].reshape(256, EH), wd[0, :, cols], preferred_element_type=F32)
            sums = sums + jnp.dot(act[(1,) + idx].reshape(256, EH), wd[1, :, cols], preferred_element_type=F32)
            part[p][idx] = sums.astype(BF16).reshape(4, 4, 16, CW[p])

            @pl.when(s == 0)
            def _():
                for h in range(2):
                    remote(
                        part[p].at[slab_part(p, 2, halves[h])], ra[p].at[h],
                        q3_s.at[p, h], q3_r.at[p, h], near(p, 2, 1 if h == 0 else 3),
                    ).start()

            @pl.when(s == 1)
            def _():
                remote(
                    part[p].at[slab_part(p, 1, halves[1])], rx[p].at[0, 1],
                    q3_s.at[p, 2], q3_r.at[p, 2], near(p, 2, 1),
                ).start()

            @pl.when(s == 2)
            def _():
                remote(
                    part[p].at[slab_part(p, 3, halves[0])], rx[p].at[1, 0],
                    q3_s.at[p, 3], q3_r.at[p, 3], near(p, 2, 3),
                ).start()

    for p in range(3):
        arrived(ra[p].at[0], q3_s.at[p, 0], q3_r.at[p, 0])
        idx = slab_part(p, 1, halves[0])
        part[p][idx] = (part[p][idx].astype(F32) + ra[p][0].astype(F32)).astype(BF16)
        send(part[p].at[idx], rx[p].at[0, 0], q3_s.at[p, 4], q3_r.at[p, 4], near(p, 2, 1))
        arrived(ra[p].at[1], q3_s.at[p, 1], q3_r.at[p, 1])
        idx = slab_part(p, 3, halves[1])
        part[p][idx] = (part[p][idx].astype(F32) + ra[p][1].astype(F32)).astype(BF16)
        send(part[p].at[idx], rx[p].at[1, 1], q3_s.at[p, 5], q3_r.at[p, 5], near(p, 2, 3))
    for p in range(3):
        arrived(rx[p].at[0, 1], q3_s.at[p, 2], q3_r.at[p, 2])
        arrived(rx[p].at[1, 0], q3_s.at[p, 3], q3_r.at[p, 3])
        arrived(rx[p].at[0, 0], q3_s.at[p, 4], q3_r.at[p, 4])
        arrived(rx[p].at[1, 1], q3_s.at[p, 5], q3_r.at[p, 5])
        for h in range(2):
            idx = slab_part(p, 0, halves[h])
            part[p][idx] = (
                part[p][idx].astype(F32) + rx[p][0, h].astype(F32) + rx[p][1, h].astype(F32)
            ).astype(BF16)
        b = ORD[p][1]
        for k, d in enumerate(STEPS):
            line = slab_part(p, 0, slice(None), lax.rem(pos[b] + d, 4))
            send(part[p].at[line], ry[p].at[k], q1_s.at[p, 0, k], q1_r.at[p, 0, k], near(p, 1, d))
    for p in range(3):
        a, b = ORD[p][0], ORD[p][1]
        line = slab_part(p, 0, slice(None), pos[b])
        total = part[p][line].astype(F32)
        for k in range(3):
            arrived(ry[p].at[k], q1_s.at[p, 0, k], q1_r.at[p, 0, k])
            total = total + ry[p][k].astype(F32)
        part[p][line] = total.astype(BF16)
        for k, d in enumerate(STEPS):
            spot = slab_part(p, 0, lax.rem(pos[a] + d, 4), pos[b])
            send(part[p].at[spot], rz[p].at[k], q1_s.at[p, 1, k], q1_r.at[p, 1, k], near(p, 0, d))
    pieces = []
    for p in range(3):
        total = part[p][pos].astype(F32)
        for k in range(3):
            arrived(rz[p].at[k], q1_s.at[p, 1, k], q1_r.at[p, 1, k])
            total = total + rz[p][k].astype(F32)
        pieces.append(total)
    mixed = (kept[...] + jnp.concatenate(pieces, axis=1)).astype(BF16).astype(F32)
    fin_tx[...] = jnp.where(first, mixed[8:], mixed[:8])
    send(fin_tx, fin_rx, pair_s.at[4], pair_r.at[4], sib)
    out[:, own_cols] = jnp.where(first, mixed[:8], mixed[8:]).astype(BF16)
    arrived(fin_rx, pair_s.at[4], pair_r.at[4])
    out[:, other_cols] = fin_rx[...].astype(BF16)

    for copy in sends:
        copy.wait_send()

    def sent(view, ssem, rsem):
        remote(view, view, ssem, rsem, sib).wait_send()

    for p in range(3):
        for rel in range(4):
            for half in range(2):
                view = half_chunk(p, rel, pos[ORD[p][2]], half)
                sent(view, g3_s.at[p, rel, 2 + half], g3_r.at[p, rel, 2 + half])
        for d in range(4):
            sent(block(p, slab(p, 0)), d_s.at[p, d], d_r.at[p, d])
    for ix in range(4):
        sent(act.at[c, ix], act_s.at[ix], act_r.at[ix])
    for p in range(3):
        for k, d in enumerate((2, 2, 1, 3)):
            sent(part[p].at[slab_part(p, d, halves[0])], q3_s.at[p, k], q3_r.at[p, k])


def local(
    residual, queries, key_cache, value_cache, new_keys, new_values, lengths, out_weight, norm_gain,
    routes, gate_probs, w_gate, w_up, w_down,
):
    vm = pl.BlockSpec(memory_space=pltpu.VMEM)
    hbm = pl.BlockSpec(memory_space=pl.ANY)
    dma = pltpu.SemaphoreType.DMA

    def v(*shape, dtype=BF16):
        return pltpu.VMEM(shape, dtype)

    def slab_shape(p, first, second):
        spec = {ORD[p][0]: first, ORD[p][1]: second}
        return tuple(spec[axis] for axis in range(3) if axis != ORD[p][2])

    scratch = [
        v(ROWS, CACHE, KVH * HD), v(ROWS, CACHE, KVH * HD), v(1024, HALF), v(D, 2 * EH), v(2, EH, HALF),
        v(8, 64, HD), v(8, 2, 64, HD), v(128, 1024), v(8, 16, HALF), v(8, 16, HALF),
        v(8, HALF, dtype=F32), v(8, HALF, dtype=F32), v(16, 128, dtype=F32), v(16, 128, dtype=F32),
        v(4, 4, 4, 2, 8, 128, dtype=F32),
        *[v(2, 4, 4, 4, 16, w) for w in CW],
        v(4, 4, 4, 16, 2 * EH, dtype=F32), v(2, 4, 4, 4, 16, EH),
        *[v(4, 4, 4, 16, w) for w in CW],
        *[v(2, *slab_shape(p, 2, 4), 16, CW[p]) for p in range(3)],
        *[v(2, 2, *slab_shape(p, 2, 4), 16, CW[p]) for p in range(3)],
        *[v(3, 4, 16, w) for w in CW],
        *[v(3, 16, w) for w in CW],
        v(16, HALF, dtype=F32), v(8, HALF, dtype=F32), v(8, HALF, dtype=F32),
        dma((7,)), dma((5,)), dma((5,)), dma((8,)), dma((8,)), dma((8,)), dma((8,)), dma((4, 8)), dma((4, 8)),
        dma((3, 3)), dma((3, 3)),
        dma((3, 2, 3)), dma((3, 2, 3)), dma((3, 4, 4)), dma((3, 4, 4)), dma((3, 4)), dma((3, 4)),
        dma((4,)), dma((4,)), dma((3, 6)), dma((3, 6)), dma((3, 2, 3)), dma((3, 2, 3)),
    ]
    return pl.pallas_call(
        kernel,
        out_shape=jax.ShapeDtypeStruct((ROWS, D), BF16),
        in_specs=[vm, vm, hbm, hbm, vm, vm, pl.BlockSpec(memory_space=pltpu.SMEM), hbm, vm, vm, vm, hbm, hbm, hbm],
        out_specs=vm,
        scratch_shapes=scratch,
        compiler_params=pltpu.CompilerParams(
            collective_id=0, has_side_effects=True, vmem_limit_bytes=58 * 2**20
        ),
        cost_estimate=pl.CostEstimate(flops=12 * 10**9, bytes_accessed=24 * 2**20, transcendentals=10**6),
    )(
        residual, queries, key_cache, value_cache, new_keys, new_values, lengths, out_weight,
        norm_gain.reshape(1, D), routes, gate_probs, w_gate, w_up, w_down,
    )


def solution(mesh):
    both = ("wide", "narrow")
    rows, cubes = P(both, None), P(both, None, None)
    in_specs = (
        rows, rows, cubes, cubes, rows, rows, P(both), P("narrow", None), P(), rows, rows, cubes, cubes, cubes,
    )
    return jax.shard_map(local, mesh=mesh, in_specs=in_specs, out_specs=rows, check_vma=False)
```

```python
import functools

import jax
import jax.numpy as jnp
from jax import lax
from jax.experimental import pallas as pl
from jax.experimental.pallas import tpu as pltpu
from jax.sharding import PartitionSpec as P

MESH = pl.DeviceIdType.MESH
F32 = jnp.float32
BF16 = jnp.bfloat16

D = 4096
HALF = 2048
HQ = 64
KVH = 4
HD = 128
TOP = 8
CACHE = 256
ROWS = 8
EH = 384

CW = (640, 640, 768)
OFF = (0, 640, 1280)
ORD = ((0, 1, 2), (1, 2, 0), (2, 0, 1))
STEPS = (1, 3, 2)


def coords():
    w, n = lax.axis_index("wide"), lax.axis_index("narrow")
    c = lax.rem(w, 2)
    z = lax.rem(lax.div(w, 2), 4)
    x = lax.div(n, 4) * 2 + lax.div(w, 8)
    return (x, lax.rem(n, 4), z), c, w * 8 + n, n


def device(pos, c):
    x, y, z = pos
    return (lax.rem(x, 2) * 8 + z * 2 + c, lax.div(x, 2) * 4 + y)


def shift(pos, axis, d):
    moved = list(pos)
    moved[axis] = lax.rem(moved[axis] + d, 4)
    return tuple(moved)


def remote(src, dst, ssem, rsem, target):
    return pltpu.make_async_remote_copy(
        src_ref=src, dst_ref=dst, send_sem=ssem, recv_sem=rsem, device_id=target, device_id_type=MESH
    )


def slab_index(p, first=slice(None), second=slice(None)):
    order = ORD[p]
    spec = {order[0]: first, order[1]: second}
    return tuple(spec[axis] for axis in range(3) if axis != order[2])


def kernel(
    residual_in, queries_in, key_cache, value_cache, new_keys_in, new_values_in, lengths_in, out_weight, gain_in,
    routes_in, probs_in, w_gate, w_up, w_down,
    out,
    residual, queries, new_keys, new_values, lengths, norm_gain, routes, gate_probs,
    keys, values, wo, wgu, wd, att, att_rx, a_mat, y_tx, y_rx, res_tx, res_rx, sq_tx, sq_rx,
    table, plane0, plane1, plane2, sel, perm, unperm, weight, stx0, stx1, stx2, srx0, srx1, srx2, acc, act,
    utx0, utx1, utx2, urx0, urx1, urx2, ltx0, ltx1, ltx2, lrx0, lrx1, lrx2, line0, line1, line2,
    btx0, btx1, btx2, brx0, brx1, brx2, kept, fin_tx, fin_rx,
    lsem, small, pair_s, pair_r, a2a_s, a2a_r, af_s, af_r, y_s, y_r, sh_s, sh_r,
    g1_s, g1_r, g2_s, g2_r, g3_s, g3_r, q3_s, q3_r, q2_s, q2_r, q1_s, q1_r,
):
    pos, c, me, n_me = coords()
    x, y, z = pos
    sib = device(pos, 1 - c)
    plane = (plane0, plane1, plane2)
    stx, srx, utx, urx = (stx0, stx1, stx2), (srx0, srx1, srx2), (utx0, utx1, utx2), (urx0, urx1, urx2)
    ltx, lrx, line = (ltx0, ltx1, ltx2), (lrx0, lrx1, lrx2), (line0, line1, line2)
    btx, brx = (btx0, btx1, btx2), (brx0, brx1, brx2)
    own_cols = pl.ds(pl.multiple_of(c * HALF, HALF), HALF)
    other_cols = pl.ds(pl.multiple_of((1 - c) * HALF, HALF), HALF)
    sends = []

    def send(src, dst, ssem, rsem, target, keep=True):
        copy = remote(src, dst, ssem, rsem, target)
        copy.start()
        if keep:
            sends.append(copy)

    def arrived(dst, ssem, rsem):
        remote(dst, dst, ssem, rsem, sib).wait_recv()

    group = [(dx, dy) for dx in range(2) for dy in range(4)]

    def member(dx, dy):
        gx = x if dx == 0 else 3 - x
        gy = lax.rem(y + dy, 4)
        return (gx, gy, z), lax.div(gx, 2) * 4 + gy

    local = [
        pltpu.make_async_copy(key_cache, keys, lsem.at[0]),
        pltpu.make_async_copy(value_cache, values, lsem.at[1]),
        pltpu.make_async_copy(out_weight.at[:, own_cols], wo, lsem.at[2]),
        pltpu.make_async_copy(w_gate.at[0], wgu.at[:, pl.ds(0, EH)], lsem.at[3]),
        pltpu.make_async_copy(w_up.at[0], wgu.at[:, pl.ds(EH, EH)], lsem.at[4]),
        pltpu.make_async_copy(w_down.at[0], wd, lsem.at[5]),
    ]
    arguments = [
        pltpu.make_async_copy(src, dst, small.at[i])
        for i, (src, dst) in enumerate((
            (routes_in, routes), (probs_in, gate_probs), (residual_in, residual), (lengths_in, lengths),
            (queries_in, queries), (new_keys_in, new_keys), (new_values_in, new_values), (gain_in, norm_gain),
        ))
    ]
    for copy in arguments:
        copy.start()
    for copy in local[:3]:
        copy.start()

    barrier = pltpu.get_barrier_semaphore()
    partners = [sib] + [device(shift(pos, a, d), c) for a in range(3) for d in STEPS]
    partners += [device(shift(pos, a, d), 1 - c) for a in range(3) for d in STEPS]
    partners += [device(member(1, dy)[0], c) for dy in (1, 2, 3)]
    for partner in partners:
        pl.semaphore_signal(barrier, inc=1, device_id=partner, device_id_type=MESH)

    for copy in arguments[:3]:
        copy.wait()
    probs = gate_probs[...]
    shares = probs / jnp.sum(probs, axis=-1, keepdims=True)
    lanes = lax.broadcasted_iota(jnp.int32, (ROWS, 128), 1)
    dense = jnp.zeros((ROWS, 128), F32)
    named = jnp.zeros((ROWS, 128), F32)
    chosen = routes[...]
    for k in range(TOP):
        hit = chosen[:, k : k + 1] == lanes
        dense = dense + jnp.where(hit, shares[:, k : k + 1], 0.0)
        named = named + jnp.where(hit, 1.0, 0.0)
    earlier, running = [], jnp.zeros((1, 128), F32)
    for t in range(ROWS):
        earlier.append(running)
        running = running + named[t : t + 1]
    earlier = jnp.concatenate(earlier, axis=0)
    number = lax.broadcasted_iota(jnp.int32, (ROWS, 128), 0).astype(F32) + 1.0
    entries = []
    for value in (number, dense):
        for r in range(2):
            taken = jnp.where(earlier == float(r), named * value, 0.0)
            entries.append(jnp.sum(taken, axis=0, keepdims=True) - (1.0 if value is number else 0.0))
    table[x, y, z, c] = jnp.concatenate(entries + [jnp.zeros((4, 128), F32)], axis=0)
    res_tx[...] = residual[:, other_cols].astype(F32)


    local[0].wait()
    local[1].wait()
    for copy in local[3:]:
        copy.start()
    for copy in arguments[3:]:
        copy.wait()
    scaling = HD ** (-0.5)
    row_request = lax.rem(lax.broadcasted_iota(jnp.int32, (128, CACHE), 0), ROWS)
    limit = jnp.zeros((128, CACHE), jnp.int32)
    for r in range(ROWS):
        limit = jnp.where(row_request == r, lengths[r], limit)
    visible = lax.broadcasted_iota(jnp.int32, (128, CACHE), 1) < limit
    for g in range(KVH):
        cols = slice(g * HD, (g + 1) * HD)
        q = jnp.concatenate(
            [queries[:, (g * 16 + h) * HD : (g * 16 + h + 1) * HD].astype(F32) for h in range(16)], axis=0
        )
        scores = lax.dot_general(
            q.astype(BF16), keys[:, :, cols].reshape(ROWS * CACHE, HD), (((1,), (1,)), ((), ())),
            preferred_element_type=F32,
        )
        picked = scores[:, :CACHE]
        for r in range(1, ROWS):
            picked = jnp.where(row_request == r, scores[:, r * CACHE : (r + 1) * CACHE], picked)
        picked = jnp.where(visible, picked * scaling, -jnp.inf)
        fresh = jnp.concatenate([new_keys[:, cols].astype(F32)] * 16, axis=0)
        own = jnp.sum(q * fresh, axis=-1, keepdims=True) * scaling
        highest = jnp.maximum(jnp.max(picked, axis=-1, keepdims=True), own)
        weights = jnp.exp(picked - highest)
        own = jnp.exp(own - highest)
        norm = jnp.sum(weights, axis=-1, keepdims=True) + own
        weights = weights / norm
        own = (own / norm).astype(BF16).astype(F32)
        spread = jnp.concatenate(
            [jnp.where(row_request == r, weights, 0.0).astype(BF16) for r in range(ROWS)], axis=1
        )
        got = jnp.dot(spread, values[:, :, cols].reshape(ROWS * CACHE, HD), preferred_element_type=F32)
        got = got + own * jnp.concatenate([new_values[:, cols].astype(F32)] * 16, axis=0)
        att[2 * g : 2 * g + 2] = got.astype(BF16).reshape(2, 64, HD)

    pl.semaphore_wait(barrier, len(partners))
    mine = pltpu.make_async_copy(att.at[n_me], att_rx.at[n_me, c], lsem.at[6])
    mine.start()
    for i, (dx, dy) in enumerate(group):
        if i:
            target, n = member(dx, dy)
            send(att.at[n], att_rx.at[n_me, c], a2a_s.at[i], a2a_r.at[i], device(target, c))
    send(res_tx, res_rx, pair_s.at[0], pair_r.at[0], sib)
    for k, d in enumerate(STEPS):
        view = table.at[x, y, z, c]
        send(view, view, sh_s.at[0, k], sh_r.at[0, k], device(shift(pos, 0, d), c))
    mine.wait()
    for i, (dx, dy) in enumerate(group):
        _, n = member(dx, (4 - dy) % 4)
        view = att_rx.at[n, c]
        if i:
            arrived(view, a2a_s.at[i], a2a_r.at[i])
        send(view, view, af_s.at[i], af_r.at[i], sib)
    for i, (dx, dy) in enumerate(group):
        _, n = member(dx, (4 - dy) % 4)
        arrived(att_rx.at[n, 1 - c], af_s.at[i], af_r.at[i])

    for k, d in enumerate(STEPS):
        view = table.at[lax.rem(x + 4 - d, 4), y, z, c]
        arrived(view, sh_s.at[0, k], sh_r.at[0, k])
    for k, d in enumerate(STEPS):
        view = table.at[:, y, z, c]
        send(view, view, sh_s.at[1, k], sh_r.at[1, k], device(shift(pos, 1, d), c))
    heads = att_rx[...].astype(F32).reshape(16, 64, HD)
    for h in range(8):
        a_mat[:, h * HD : (h + 1) * HD] = heads[:, h * 8 : (h + 1) * 8].reshape(128, HD).astype(BF16)

    local[2].wait()
    for j in range(4):
        cols = pl.ds(j * 512, 512)
        sums = jnp.dot(a_mat[...], wo[:, cols], preferred_element_type=F32)
        y_tx[:, :, cols] = sums.astype(BF16).reshape(8, 16, 512)
        for i, (dx, dy) in enumerate(group):
            if i:
                target, n = member(dx, dy)
                send(y_tx.at[n, :, cols], y_rx.at[i, :, cols], y_s.at[j, i], y_r.at[j, i], device(target, c))
    for k, d in enumerate(STEPS):
        view = table.at[:, lax.rem(y + 4 - d, 4), z, c]
        arrived(view, sh_s.at[1, k], sh_r.at[1, k])
    for k, d in enumerate(STEPS):
        view = table.at[:, :, z, c]
        send(view, view, sh_s.at[2, k], sh_r.at[2, k], device(shift(pos, 2, d), c))

    big_r = lax.broadcasted_iota(jnp.int32, (256, 256), 0)
    big_c = lax.broadcasted_iota(jnp.int32, (256, 256), 1)

    def common(i, p):
        digits = {ORD[p][2]: lax.div(i, 64), ORD[p][1]: lax.rem(lax.div(i, 16), 4), ORD[p][0]: lax.rem(lax.div(i, 4), 4)}
        return digits[2] * 64 + digits[1] * 16 + digits[0] * 4 + lax.rem(i, 4)

    for p in (1, 2):
        perm[p - 1] = jnp.where(big_r == common(big_c, p), 1.0, 0.0).astype(BF16)
        unperm[p - 1] = jnp.where(common(big_r, p) == big_c, 1.0, 0.0).astype(BF16)
    arrived(res_rx, pair_s.at[0], pair_r.at[0])
    own_res, other_res = residual[:, own_cols].astype(F32), res_rx[...]
    first = c == 0
    total = jnp.concatenate(
        [jnp.where(first, own_res, other_res), jnp.where(first, other_res, own_res)], axis=0
    )
    attention = y_tx[n_me].astype(F32)
    for i in range(1, 8):
        for j in range(4):
            arrived(y_rx.at[i, :, pl.ds(j * 512, 512)], y_s.at[j, i], y_r.at[j, i])
        attention = attention + y_rx[i].astype(F32)
    for k, d in enumerate(STEPS):
        view = table.at[:, :, lax.rem(z + 4 - d, 4), c]
        arrived(view, sh_s.at[2, k], sh_r.at[2, k])
    view = table.at[:, :, :, c]
    send(view, view, pair_s.at[3], pair_r.at[3], sib)
    stream = (total + attention).astype(BF16).astype(F32)
    squares = jnp.sum(stream * stream, axis=-1, keepdims=True)
    sq_tx[...] = jnp.broadcast_to(squares, (16, 128))
    send(sq_tx, sq_rx, pair_s.at[2], pair_r.at[2], sib)
    kept[...] = stream
    arrived(sq_rx, pair_s.at[2], pair_r.at[2])
    mean = (squares + sq_rx[:, 0:1]) * (1.0 / D)
    normed = (stream * lax.rsqrt(mean + 1e-06) * norm_gain[:, own_cols]).astype(BF16)
    for p in range(3):
        plane[p][slab_index(p, pos[ORD[p][0]], pos[ORD[p][1]])] = normed[:, OFF[p] : OFF[p] + CW[p]]

    def at(p, first, second):
        return plane[p].at[slab_index(p, first, second)]

    def near(p, stage, d, core=c):
        return device(shift(pos, ORD[p][stage], d), core)

    def coordinate(p, stage, d):
        return lax.rem(pos[ORD[p][stage]] + d, 4)

    def along(p, i, d):
        return coordinate(p, 0, 0 if i == 0 else 4 - STEPS[i - 1]), coordinate(p, 1, d)

    def spread_block(p, i):
        view = at(p, *along(p, i, 0))
        for k, d in enumerate(STEPS):
            send(view, view, g2_s.at[p, i, k], g2_r.at[p, i, k], near(p, 1, d))

    for p in range(3):
        view = at(p, *along(p, 0, 0))
        for k, d in enumerate(STEPS):
            send(view, view, g1_s.at[p, k], g1_r.at[p, k], near(p, 0, d))
    for p in range(3):
        spread_block(p, 0)

    arrived(table.at[:, :, :, 1 - c], pair_s.at[3], pair_r.at[3])
    slot = lax.broadcasted_iota(jnp.int32, (16, 64), 0)
    token = lax.broadcasted_iota(jnp.int32, (16, 64), 1)
    same = lax.div(slot, 2) == lax.div(token, 8)
    place = lax.rem(token, 8)
    take_token = jnp.where(same & (place == lax.rem(slot, 2)), 1.0, 0.0).astype(BF16)
    take_share = jnp.where(same & (place == lax.rem(slot, 2) + 2), 1.0, 0.0).astype(BF16)
    place = place.astype(F32)
    lane16 = lax.broadcasted_iota(jnp.int32, (16, 128), 1)

    def expert_of(where, core):
        ex, ey, ez = where
        return lax.div(((lax.rem(ex, 2) * 8 + ez * 2 + core) * 8) + lax.div(ex, 2) * 4 + ey, 2)

    for p in range(3):
        for rel in range(4):
            idx = list(pos)
            idx[ORD[p][0]], idx[ORD[p][1]] = slice(None), coordinate(p, 1, rel)
            entries = table[tuple(idx)].reshape(64, 128).astype(BF16)
            numbers = jnp.dot(take_token, entries, preferred_element_type=F32)
            for q in range(4):
                chip = list(pos)
                chip[ORD[p][2]] = q
                for core in range(2):
                    wanted = jnp.sum(
                        jnp.where(lane16 == expert_of(chip, core), numbers, 0.0), axis=-1, keepdims=True
                    )
                    hits = jnp.where(same & (wanted == place), 1.0, 0.0)
                    sel[p, rel, (q * 2 + core) * 16 : (q * 2 + core + 1) * 16] = hits.astype(BF16)

    def dispatch(p, rel):
        rows = plane[p][slab_index(p, slice(None), coordinate(p, 1, rel))].reshape(64, CW[p])
        picked = jnp.dot(sel[p, rel], rows, preferred_element_type=F32).astype(BF16)
        stx[p][rel] = picked.reshape(4, 2, 16, CW[p])
        a3, a2 = coordinate(p, 2, 0), coordinate(p, 1, rel)
        spot = srx[p].at[c, a3, a2]
        for dq in STEPS:
            for core in range(2):
                send(
                    stx[p].at[rel, coordinate(p, 2, dq), core], spot,
                    g3_s.at[p, rel, dq, core], g3_r.at[p, rel, dq, c], near(p, 2, dq, core),
                )
        send(stx[p].at[rel, a3, 1 - c], spot, g3_s.at[p, rel, 0, 0], g3_r.at[p, rel, 0, 0], sib)
        srx[p][c, a3, a2] = stx[p][rel, a3, c]

    for k, d in enumerate(STEPS):
        for p in range(3):
            arrived(at(p, *along(p, k + 1, 0)), g1_s.at[p, k], g1_r.at[p, k])
            spread_block(p, k + 1)
    for p in range(3):
        dispatch(p, 0)
    for k, d in enumerate(STEPS):
        for p in range(3):
            for i in range(4):
                arrived(at(p, *along(p, i, 4 - d)), g2_s.at[p, i, k], g2_r.at[p, i, k])
            dispatch(p, 4 - d)

    mine_expert = lax.div(me, 2)

    @pl.loop(0, 16)
    def _(i):
        entries = table[:, lax.rem(i, 4), lax.div(i, 4)].reshape(64, 128)
        high = entries.astype(BF16)
        low = (entries - high.astype(F32)).astype(BF16)
        values = jnp.dot(take_share, high, preferred_element_type=F32)
        values = values + jnp.dot(take_share, low, preferred_element_type=F32)
        found = jnp.sum(jnp.where(lane16 == mine_expert, values, 0.0), axis=-1, keepdims=True)
        weight[i] = jnp.broadcast_to(found, (16, 128))

    for copy in local[3:]:
        copy.wait()

    for p in range(3):
        for rel in (0, 3, 1, 2):
            a2 = coordinate(p, 1, rel)
            for dq in STEPS:
                for core in range(2):
                    arrived(
                        srx[p].at[core, coordinate(p, 2, 4 - dq), a2],
                        g3_s.at[p, rel, dq, core], g3_r.at[p, rel, dq, core],
                    )
            arrived(srx[p].at[1 - c, coordinate(p, 2, 0), a2], g3_s.at[p, rel, 0, 0], g3_r.at[p, rel, 0, 0])
        for half in range(2):
            rows = srx[p][half].reshape(256, CW[p])
            if p:
                rows = jnp.dot(perm[p - 1], rows, preferred_element_type=F32).astype(BF16)
            k = slice(half * HALF + OFF[p], half * HALF + OFF[p] + CW[p])
            sums = jnp.dot(rows, wgu[k, :], preferred_element_type=F32)
            acc[...] = sums if p == 0 and half == 0 else acc[...] + sums
    gate, up = acc[:, :EH], acc[:, EH:]
    shares = weight[...].reshape(256, 128)[:, 0:1]
    active = (gate / (1.0 + jnp.exp(-gate)) * up * shares).astype(BF16)
    act[0] = active
    for p in (1, 2):
        act[p] = jnp.dot(unperm[p - 1], active, preferred_element_type=F32).astype(BF16)

    def give_back(p, half, rel):
        a3, a2 = coordinate(p, 2, 0), coordinate(p, 1, rel)
        spot = urx[p].at[a2, a3, c]
        for dq in STEPS:
            send(
                utx[p].at[half, coordinate(p, 2, dq), a2], spot,
                q3_s.at[p, rel, dq, half], q3_r.at[p, rel, dq, c], near(p, 2, dq, half),
            )

    for half in range(2):
        for p in range(3):
            cols = slice(half * HALF + OFF[p], half * HALF + OFF[p] + CW[p])
            sums = jnp.dot(act[p], wd[:, cols], preferred_element_type=F32)
            utx[p][half] = sums.astype(BF16).reshape(4, 4, 16, CW[p])
            give_back(p, half, 2)
    for rel in (2, 1, 3, 0):
        for p in range(3):
            a3, a2 = coordinate(p, 2, 0), coordinate(p, 1, rel)
            if rel != 2:
                for half in range(2):
                    give_back(p, half, rel)
            send(utx[p].at[1 - c, a3, a2], urx[p].at[a2, a3, c], q3_s.at[p, rel, 0, 0], q3_r.at[p, rel, 0, 0], sib)
            urx[p][a2, a3, c] = utx[p][c, a3, a2]

    for rel in (2, 1, 3, 0):
        for p in range(3):
            a2 = coordinate(p, 1, rel)
            for dq in STEPS:
                for core in range(2):
                    arrived(
                        urx[p].at[a2, coordinate(p, 2, 4 - dq), core],
                        q3_s.at[p, rel, dq, core], q3_r.at[p, rel, dq, core],
                    )
            arrived(urx[p].at[a2, coordinate(p, 2, 0), 1 - c], q3_s.at[p, rel, 0, 0], q3_r.at[p, rel, 0, 0])
            sums = lax.dot_general(
                sel[p, rel], urx[p][a2].reshape(128, CW[p]), (((0,), (0,)), ((), ())), preferred_element_type=F32
            )
            if rel:
                ltx[p][rel - 1] = sums.astype(BF16).reshape(4, 16, CW[p])
                send(ltx[p].at[rel - 1], lrx[p].at[rel - 1], q2_s.at[p, rel - 1], q2_r.at[p, rel - 1], near(p, 1, rel))
            else:
                line[p][...] = sums.reshape(4, 16, CW[p])
    for p in range(3):
        total = line[p][...]
        for k in (1, 0, 2):
            arrived(lrx[p].at[k], q2_s.at[p, k], q2_r.at[p, k])
            total = total + lrx[p][k].astype(F32)
        line[p][...] = total
        btx[p][...] = total.astype(BF16)
        for k, d in enumerate(STEPS):
            send(btx[p].at[coordinate(p, 0, d)], brx[p].at[k], q1_s.at[p, k], q1_r.at[p, k], near(p, 0, d))
    pieces = []
    for p in range(3):
        total = line[p][coordinate(p, 0, 0)]
        for k in range(3):
            arrived(brx[p].at[k], q1_s.at[p, k], q1_r.at[p, k])
            total = total + brx[p][k].astype(F32)
        pieces.append(total)
    mixed = (kept[...] + jnp.concatenate(pieces, axis=1)).astype(BF16).astype(F32)
    fin_tx[...] = jnp.where(first, mixed[8:], mixed[:8])
    send(fin_tx, fin_rx, pair_s.at[4], pair_r.at[4], sib)
    out[:, own_cols] = jnp.where(first, mixed[:8], mixed[8:]).astype(BF16)
    arrived(fin_rx, pair_s.at[4], pair_r.at[4])
    out[:, other_cols] = fin_rx[...].astype(BF16)

    for copy in sends:
        copy.wait_send()


def local(
    residual, queries, key_cache, value_cache, new_keys, new_values, lengths, out_weight, norm_gain,
    routes, gate_probs, w_gate, w_up, w_down,
):
    vm = pl.BlockSpec(memory_space=pltpu.VMEM)
    hbm = pl.BlockSpec(memory_space=pl.ANY)
    dma = pltpu.SemaphoreType.DMA

    def v(*shape, dtype=BF16):
        return pltpu.VMEM(shape, dtype)

    scratch = [
        v(ROWS, D), v(ROWS, HQ * HD), v(ROWS, KVH * HD), v(ROWS, KVH * HD), pltpu.SMEM((ROWS,), jnp.int32),
        v(1, D, dtype=F32), v(ROWS, TOP, dtype=jnp.int32), v(ROWS, TOP, dtype=F32),
        v(ROWS, CACHE, KVH * HD), v(ROWS, CACHE, KVH * HD), v(1024, HALF), v(D, 2 * EH), v(EH, D),
        v(8, 64, HD), v(8, 2, 64, HD), v(128, 1024), v(8, 16, HALF), v(8, 16, HALF),
        v(8, HALF, dtype=F32), v(8, HALF, dtype=F32), v(16, 128, dtype=F32), v(16, 128, dtype=F32),
        v(4, 4, 4, 2, 8, 128, dtype=F32),
        *[v(4, 4, 16, w) for w in CW],
        v(3, 4, 128, 64), v(2, 256, 256), v(2, 256, 256), v(16, 16, 128, dtype=F32),
        *[v(4, 4, 2, 16, w) for w in CW],
        *[v(2, 4, 4, 16, w) for w in CW],
        v(256, 2 * EH, dtype=F32), v(3, 256, EH),
        *[v(2, 4, 4, 16, w) for w in CW],
        *[v(4, 4, 2, 16, w) for w in CW],
        *[v(3, 4, 16, w) for w in CW],
        *[v(3, 4, 16, w) for w in CW],
        *[v(4, 16, w, dtype=F32) for w in CW],
        *[v(4, 16, w) for w in CW],
        *[v(3, 16, w) for w in CW],
        v(16, HALF, dtype=F32), v(8, HALF, dtype=F32), v(8, HALF, dtype=F32),
        dma((7,)), dma((8,)), dma((5,)), dma((5,)), dma((8,)), dma((8,)), dma((8,)), dma((8,)), dma((4, 8)), dma((4, 8)),
        dma((3, 3)), dma((3, 3)), dma((3, 3)), dma((3, 3)), dma((3, 4, 3)), dma((3, 4, 3)),
        dma((3, 4, 4, 2)), dma((3, 4, 4, 2)), dma((3, 4, 4, 2)), dma((3, 4, 4, 2)),
        dma((3, 3)), dma((3, 3)), dma((3, 3)), dma((3, 3)),
    ]
    return pl.pallas_call(
        kernel,
        out_shape=jax.ShapeDtypeStruct((ROWS, D), BF16),
        in_specs=[hbm] * 14,
        out_specs=vm,
        scratch_shapes=scratch,
        compiler_params=pltpu.CompilerParams(
            collective_id=0, has_side_effects=True, vmem_limit_bytes=58 * 2**20
        ),
        cost_estimate=pl.CostEstimate(flops=12 * 10**9, bytes_accessed=24 * 2**20, transcendentals=10**6),
    )(
        residual, queries, key_cache, value_cache, new_keys, new_values, lengths, out_weight,
        norm_gain.reshape(1, D), routes, gate_probs, w_gate, w_up, w_down,
    )


def solution(mesh):
    both = ("wide", "narrow")
    rows, cubes = P(both, None), P(both, None, None)
    in_specs = (
        rows, rows, cubes, cubes, rows, rows, P(both), P("narrow", None), P(), rows, rows, cubes, cubes, cubes,
    )
    return jax.shard_map(local, mesh=mesh, in_specs=in_specs, out_specs=rows, check_vma=False)
```

```python
import functools

import jax
import jax.numpy as jnp
from jax import lax
from jax.experimental import pallas as pl
from jax.experimental.pallas import tpu as pltpu
from jax.sharding import PartitionSpec as P

MESH = pl.DeviceIdType.MESH
F32 = jnp.float32
BF16 = jnp.bfloat16

D = 4096
HALF = 2048
HQ = 64
KVH = 4
HD = 128
TOP = 8
CACHE = 256
ROWS = 8
EH = 384

CW = (640, 640, 768)
OFF = (0, 640, 1280)
ORD = ((0, 1, 2), (1, 2, 0), (2, 0, 1))
STEPS = (1, 3, 2)


def coords():
    w, n = lax.axis_index("wide"), lax.axis_index("narrow")
    c = lax.rem(w, 2)
    z = lax.rem(lax.div(w, 2), 4)
    x = lax.div(n, 4) * 2 + lax.div(w, 8)
    return (x, lax.rem(n, 4), z), c, w * 8 + n, n


def device(pos, c):
    x, y, z = pos
    return (lax.rem(x, 2) * 8 + z * 2 + c, lax.div(x, 2) * 4 + y)


def shift(pos, axis, d):
    moved = list(pos)
    moved[axis] = lax.rem(moved[axis] + d, 4)
    return tuple(moved)


def remote(src, dst, ssem, rsem, target):
    return pltpu.make_async_remote_copy(
        src_ref=src, dst_ref=dst, send_sem=ssem, recv_sem=rsem, device_id=target, device_id_type=MESH
    )


def slab_index(p, first=slice(None), second=slice(None)):
    order = ORD[p]
    spec = {order[0]: first, order[1]: second}
    return tuple(spec[axis] for axis in range(3) if axis != order[2])


def kernel(
    residual_in, queries_in, key_cache, value_cache, new_keys_in, new_values_in, lengths_in, out_weight, gain_in,
    routes_in, probs_in, w_gate, w_up, w_down,
    out,
    residual, queries, new_keys, new_values, lengths, norm_gain, routes, gate_probs,
    keys, values, wo, wgu, wd, att, att_rx, a_mat, y_tx, y_rx, res_tx, res_rx, sq_tx, sq_rx,
    table, plane0, plane1, plane2, sel, perm, unperm, weight, stx0, stx1, stx2, srx0, srx1, srx2, acc, act,
    utx0, utx1, utx2, urx0, urx1, urx2, ltx0, ltx1, ltx2, lrx0, lrx1, lrx2, line0, line1, line2,
    btx0, btx1, btx2, brx0, brx1, brx2, kept, fin_tx, fin_rx,
    lsem, small, pair_s, pair_r, a2a_s, a2a_r, af_s, af_r, y_s, y_r, sh_s, sh_r,
    g1_s, g1_r, g2_s, g2_r, g3_s, g3_r, q3_s, q3_r, q2_s, q2_r, q1_s, q1_r,
):
    pos, c, me, n_me = coords()
    x, y, z = pos
    sib = device(pos, 1 - c)
    plane = (plane0, plane1, plane2)
    stx, srx, utx, urx = (stx0, stx1, stx2), (srx0, srx1, srx2), (utx0, utx1, utx2), (urx0, urx1, urx2)
    ltx, lrx, line = (ltx0, ltx1, ltx2), (lrx0, lrx1, lrx2), (line0, line1, line2)
    btx, brx = (btx0, btx1, btx2), (brx0, brx1, brx2)
    own_cols = pl.ds(pl.multiple_of(c * HALF, HALF), HALF)
    other_cols = pl.ds(pl.multiple_of((1 - c) * HALF, HALF), HALF)
    few = pl.ds(0, 3)

    def send(src, dst, ssem, rsem, target):
        remote(src, dst, ssem, rsem, target).start()

    def sent(src, ssem):
        remote(src, src, ssem, ssem, sib).wait_send()

    def arrived(dst, ssem, rsem):
        remote(dst, dst, ssem, rsem, sib).wait_recv()

    group = [(dx, dy) for dx in range(2) for dy in range(4)]

    def member(dx, dy):
        gx = x if dx == 0 else 3 - x
        gy = lax.rem(y + dy, 4)
        return (gx, gy, z), lax.div(gx, 2) * 4 + gy

    local = [
        pltpu.make_async_copy(key_cache, keys, lsem.at[0]),
        pltpu.make_async_copy(value_cache, values, lsem.at[1]),
        pltpu.make_async_copy(out_weight.at[:, own_cols], wo, lsem.at[2]),
        pltpu.make_async_copy(w_gate.at[0], wgu.at[:, pl.ds(0, EH)], lsem.at[3]),
        pltpu.make_async_copy(w_up.at[0], wgu.at[:, pl.ds(EH, EH)], lsem.at[4]),
        pltpu.make_async_copy(w_down.at[0], wd, lsem.at[5]),
    ]
    arguments = [
        pltpu.make_async_copy(src, dst, small.at[i])
        for i, (src, dst) in enumerate((
            (lengths_in, lengths), (queries_in, queries), (new_keys_in, new_keys), (new_values_in, new_values),
            (routes_in, routes), (probs_in, gate_probs), (residual_in, residual), (gain_in, norm_gain),
        ))
    ]
    for copy in arguments:
        copy.start()
    for copy in local[:3]:
        copy.start()

    barrier = pltpu.get_barrier_semaphore()
    partners = [sib] + [device(shift(pos, a, d), c) for a in range(3) for d in STEPS]
    partners += [device(shift(pos, a, d), 1 - c) for a in range(3) for d in STEPS]
    partners += [device(member(1, dy)[0], c) for dy in (1, 2, 3)]
    for partner in partners:
        pl.semaphore_signal(barrier, inc=1, device_id=partner, device_id_type=MESH)


    local[0].wait()
    local[1].wait()
    for copy in local[3:]:
        copy.start()
    for copy in arguments[:4]:
        copy.wait()
    scaling = HD ** (-0.5)
    row_request = lax.rem(lax.broadcasted_iota(jnp.int32, (128, CACHE), 0), ROWS)
    limit = jnp.zeros((128, CACHE), jnp.int32)
    for r in range(ROWS):
        limit = jnp.where(row_request == r, lengths[r], limit)
    visible = lax.broadcasted_iota(jnp.int32, (128, CACHE), 1) < limit
    for g in range(KVH):
        cols = slice(g * HD, (g + 1) * HD)
        q = jnp.concatenate(
            [queries[:, (g * 16 + h) * HD : (g * 16 + h + 1) * HD].astype(F32) for h in range(16)], axis=0
        )
        scores = lax.dot_general(
            q.astype(BF16), keys[:, :, cols].reshape(ROWS * CACHE, HD), (((1,), (1,)), ((), ())),
            preferred_element_type=F32,
        )
        picked = scores[:, :CACHE]
        for r in range(1, ROWS):
            picked = jnp.where(row_request == r, scores[:, r * CACHE : (r + 1) * CACHE], picked)
        picked = jnp.where(visible, picked * scaling, -jnp.inf)
        fresh = jnp.concatenate([new_keys[:, cols].astype(F32)] * 16, axis=0)
        own = jnp.sum(q * fresh, axis=-1, keepdims=True) * scaling
        highest = jnp.maximum(jnp.max(picked, axis=-1, keepdims=True), own)
        weights = jnp.exp(picked - highest)
        own = jnp.exp(own - highest)
        norm = jnp.sum(weights, axis=-1, keepdims=True) + own
        weights = weights / norm
        own = (own / norm).astype(BF16).astype(F32)
        spread = jnp.concatenate(
            [jnp.where(row_request == r, weights, 0.0).astype(BF16) for r in range(ROWS)], axis=1
        )
        got = jnp.dot(spread, values[:, :, cols].reshape(ROWS * CACHE, HD), preferred_element_type=F32)
        got = got + own * jnp.concatenate([new_values[:, cols].astype(F32)] * 16, axis=0)
        att[2 * g : 2 * g + 2] = got.astype(BF16).reshape(2, 64, HD)

    pl.semaphore_wait(barrier, len(partners))
    mine = pltpu.make_async_copy(att.at[n_me], att_rx.at[n_me, c], lsem.at[6])
    mine.start()
    for i, (dx, dy) in enumerate(group):
        if i:
            target, n = member(dx, dy)
            send(att.at[n], att_rx.at[n_me, c], a2a_s.at[0], a2a_r.at[i], device(target, c))
    for copy in arguments[4:]:
        copy.wait()
    probs = gate_probs[...]
    shares = probs / jnp.sum(probs, axis=-1, keepdims=True)
    lanes = lax.broadcasted_iota(jnp.int32, (ROWS, 128), 1)
    dense = jnp.zeros((ROWS, 128), F32)
    named = jnp.zeros((ROWS, 128), F32)
    chosen = routes[...]
    for k in range(TOP):
        hit = chosen[:, k : k + 1] == lanes
        dense = dense + jnp.where(hit, shares[:, k : k + 1], 0.0)
        named = named + jnp.where(hit, 1.0, 0.0)
    earlier, running = [], jnp.zeros((1, 128), F32)
    for t in range(ROWS):
        earlier.append(running)
        running = running + named[t : t + 1]
    earlier = jnp.concatenate(earlier, axis=0)
    number = lax.broadcasted_iota(jnp.int32, (ROWS, 128), 0).astype(F32) + 1.0
    entries = []
    for value in (number, dense):
        for r in range(2):
            taken = jnp.where(earlier == float(r), named * value, 0.0)
            entries.append(jnp.sum(taken, axis=0, keepdims=True) - (1.0 if value is number else 0.0))
    table[x, y, z, c] = jnp.concatenate(entries + [jnp.zeros((4, 128), F32)], axis=0)
    res_tx[...] = residual[:, other_cols].astype(F32)
    send(res_tx, res_rx, pair_s.at[0], pair_r.at[0], sib)
    for d in STEPS:
        view = table.at[x, y, z, c]
        send(view, view, sh_s.at[0], sh_r.at[0], device(shift(pos, 0, d), c))
    mine.wait()
    for i, (dx, dy) in enumerate(group):
        _, n = member(dx, (4 - dy) % 4)
        view = att_rx.at[n, c]
        if i:
            arrived(view, a2a_s.at[0], a2a_r.at[i])
        send(view, view, af_s.at[0], af_r.at[0], sib)
    arrived(att_rx.at[:, 1 - c], af_s.at[0], af_r.at[0])

    arrived(table.at[few, y, z, c], sh_s.at[0], sh_r.at[0])
    for d in STEPS:
        view = table.at[:, y, z, c]
        send(view, view, sh_s.at[1], sh_r.at[1], device(shift(pos, 1, d), c))
    heads = att_rx[...].astype(F32).reshape(16, 64, HD)
    for h in range(8):
        a_mat[:, h * HD : (h + 1) * HD] = heads[:, h * 8 : (h + 1) * 8].reshape(128, HD).astype(BF16)

    local[2].wait()
    for j in range(4):
        cols = pl.ds(j * 512, 512)
        sums = jnp.dot(a_mat[...], wo[:, cols], preferred_element_type=F32)
        y_tx[:, :, cols] = sums.astype(BF16).reshape(8, 16, 512)
        for i, (dx, dy) in enumerate(group):
            if i:
                target, n = member(dx, dy)
                send(y_tx.at[n, :, cols], y_rx.at[i, :, cols], y_s.at[0], y_r.at[0], device(target, c))
    arrived(table.at[:, few, z, c], sh_s.at[1], sh_r.at[1])
    for d in STEPS:
        view = table.at[:, :, z, c]
        send(view, view, sh_s.at[2], sh_r.at[2], device(shift(pos, 2, d), c))

    big_r = lax.broadcasted_iota(jnp.int32, (256, 256), 0)
    big_c = lax.broadcasted_iota(jnp.int32, (256, 256), 1)

    def common(i, p):
        digits = {ORD[p][2]: lax.div(i, 64), ORD[p][1]: lax.rem(lax.div(i, 16), 4), ORD[p][0]: lax.rem(lax.div(i, 4), 4)}
        return digits[2] * 64 + digits[1] * 16 + digits[0] * 4 + lax.rem(i, 4)

    for p in (1, 2):
        perm[p - 1] = jnp.where(big_r == common(big_c, p), 1.0, 0.0).astype(BF16)
        unperm[p - 1] = jnp.where(common(big_r, p) == big_c, 1.0, 0.0).astype(BF16)
    arrived(res_rx, pair_s.at[0], pair_r.at[0])
    own_res, other_res = residual[:, own_cols].astype(F32), res_rx[...]
    first = c == 0
    total = jnp.concatenate(
        [jnp.where(first, own_res, other_res), jnp.where(first, other_res, own_res)], axis=0
    )
    attention = y_tx[n_me].astype(F32)
    arrived(y_rx.at[pl.ds(1, 7)], y_s.at[0], y_r.at[0])
    for i in range(1, 8):
        attention = attention + y_rx[i].astype(F32)
    arrived(table.at[:, :, few, c], sh_s.at[2], sh_r.at[2])
    view = table.at[:, :, :, c]
    send(view, view, pair_s.at[3], pair_r.at[3], sib)
    stream = (total + attention).astype(BF16).astype(F32)
    squares = jnp.sum(stream * stream, axis=-1, keepdims=True)
    sq_tx[...] = jnp.broadcast_to(squares, (16, 128))
    send(sq_tx, sq_rx, pair_s.at[2], pair_r.at[2], sib)
    kept[...] = stream
    arrived(sq_rx, pair_s.at[2], pair_r.at[2])
    mean = (squares + sq_rx[:, 0:1]) * (1.0 / D)
    normed = (stream * lax.rsqrt(mean + 1e-06) * norm_gain[:, own_cols]).astype(BF16)
    for p in range(3):
        plane[p][slab_index(p, pos[ORD[p][0]], pos[ORD[p][1]])] = normed[:, OFF[p] : OFF[p] + CW[p]]

    def at(p, first, second):
        return plane[p].at[slab_index(p, first, second)]

    def near(p, stage, d, core=c):
        return device(shift(pos, ORD[p][stage], d), core)

    def coordinate(p, stage, d):
        return lax.rem(pos[ORD[p][stage]] + d, 4)

    def along(p, i, d):
        return coordinate(p, 0, 0 if i == 0 else 4 - STEPS[i - 1]), coordinate(p, 1, d)

    def spread_block(p, i):
        view = at(p, *along(p, i, 0))
        for k, d in enumerate(STEPS):
            send(view, view, g2_s.at[p], g2_r.at[p, k], near(p, 1, d))

    for p in range(3):
        view = at(p, *along(p, 0, 0))
        for k, d in enumerate(STEPS):
            send(view, view, g1_s.at[p], g1_r.at[p, k], near(p, 0, d))
    for p in range(3):
        spread_block(p, 0)

    arrived(table.at[:, :, :, 1 - c], pair_s.at[3], pair_r.at[3])
    slot = lax.broadcasted_iota(jnp.int32, (16, 64), 0)
    token = lax.broadcasted_iota(jnp.int32, (16, 64), 1)
    same = lax.div(slot, 2) == lax.div(token, 8)
    place = lax.rem(token, 8)
    take_token = jnp.where(same & (place == lax.rem(slot, 2)), 1.0, 0.0).astype(BF16)
    take_share = jnp.where(same & (place == lax.rem(slot, 2) + 2), 1.0, 0.0).astype(BF16)
    place = place.astype(F32)
    lane16 = lax.broadcasted_iota(jnp.int32, (16, 128), 1)

    def expert_of(where, core):
        ex, ey, ez = where
        return lax.div(((lax.rem(ex, 2) * 8 + ez * 2 + core) * 8) + lax.div(ex, 2) * 4 + ey, 2)

    for p in range(3):
        for rel in range(4):
            idx = list(pos)
            idx[ORD[p][0]], idx[ORD[p][1]] = slice(None), coordinate(p, 1, rel)
            entries = table[tuple(idx)].reshape(64, 128).astype(BF16)
            numbers = jnp.dot(take_token, entries, preferred_element_type=F32)
            for q in range(4):
                chip = list(pos)
                chip[ORD[p][2]] = q
                for core in range(2):
                    wanted = jnp.sum(
                        jnp.where(lane16 == expert_of(chip, core), numbers, 0.0), axis=-1, keepdims=True
                    )
                    hits = jnp.where(same & (wanted == place), 1.0, 0.0)
                    sel[p, rel, (q * 2 + core) * 16 : (q * 2 + core + 1) * 16] = hits.astype(BF16)

    def dispatch(p, rel):
        rows = plane[p][slab_index(p, slice(None), coordinate(p, 1, rel))].reshape(64, CW[p])
        picked = jnp.dot(sel[p, rel], rows, preferred_element_type=F32).astype(BF16)
        stx[p][rel] = picked.reshape(4, 2, 16, CW[p])
        a3, a2 = coordinate(p, 2, 0), coordinate(p, 1, rel)
        spot = srx[p].at[c, a3, a2]
        for dq in STEPS:
            for core in range(2):
                send(
                    stx[p].at[rel, coordinate(p, 2, dq), core], spot,
                    g3_s.at[p, 0], g3_r.at[p, 0], near(p, 2, dq, core),
                )
        send(stx[p].at[rel, a3, 1 - c], spot, g3_s.at[p, 1], g3_r.at[p, 1], sib)
        srx[p][c, a3, a2] = stx[p][rel, a3, c]

    for k, d in enumerate(STEPS):
        for p in range(3):
            arrived(at(p, *along(p, k + 1, 0)), g1_s.at[p], g1_r.at[p, k])
            spread_block(p, k + 1)
    for p in range(3):
        dispatch(p, 0)
    for k, d in enumerate(STEPS):
        for p in range(3):
            arrived(at(p, slice(None), coordinate(p, 1, 4 - d)), g2_s.at[p], g2_r.at[p, k])
            dispatch(p, 4 - d)

    mine_expert = lax.div(me, 2)

    @pl.loop(0, 16)
    def _(i):
        entries = table[:, lax.rem(i, 4), lax.div(i, 4)].reshape(64, 128)
        high = entries.astype(BF16)
        low = (entries - high.astype(F32)).astype(BF16)
        values = jnp.dot(take_share, high, preferred_element_type=F32)
        values = values + jnp.dot(take_share, low, preferred_element_type=F32)
        found = jnp.sum(jnp.where(lane16 == mine_expert, values, 0.0), axis=-1, keepdims=True)
        weight[i] = jnp.broadcast_to(found, (16, 128))

    for copy in local[3:]:
        copy.wait()

    for p in range(3):
        arrived(srx[p].at[:, few], g3_s.at[p, 0], g3_r.at[p, 0])
        arrived(srx[p].at[0, 0], g3_s.at[p, 1], g3_r.at[p, 1])
        for half in range(2):
            rows = srx[p][half].reshape(256, CW[p])
            if p:
                rows = jnp.dot(perm[p - 1], rows, preferred_element_type=F32).astype(BF16)
            k = slice(half * HALF + OFF[p], half * HALF + OFF[p] + CW[p])
            sums = jnp.dot(rows, wgu[k, :], preferred_element_type=F32)
            acc[...] = sums if p == 0 and half == 0 else acc[...] + sums
    gate, up = acc[:, :EH], acc[:, EH:]
    shares = weight[...].reshape(256, 128)[:, 0:1]
    active = (gate / (1.0 + jnp.exp(-gate)) * up * shares).astype(BF16)
    act[0] = active
    for p in (1, 2):
        act[p] = jnp.dot(unperm[p - 1], active, preferred_element_type=F32).astype(BF16)

    def give_back(p, half, rel):
        a3, a2 = coordinate(p, 2, 0), coordinate(p, 1, rel)
        spot = urx[p].at[a2, a3, c]
        for dq in STEPS:
            send(
                utx[p].at[half, coordinate(p, 2, dq), a2], spot,
                q3_s.at[p, 0], q3_r.at[p, rel, 0], near(p, 2, dq, half),
            )

    for half in range(2):
        for p in range(3):
            cols = slice(half * HALF + OFF[p], half * HALF + OFF[p] + CW[p])
            sums = jnp.dot(act[p], wd[:, cols], preferred_element_type=F32)
            utx[p][half] = sums.astype(BF16).reshape(4, 4, 16, CW[p])
            give_back(p, half, 2)
    for rel in (2, 1, 3, 0):
        for p in range(3):
            a3, a2 = coordinate(p, 2, 0), coordinate(p, 1, rel)
            if rel != 2:
                for half in range(2):
                    give_back(p, half, rel)
            send(utx[p].at[1 - c, a3, a2], urx[p].at[a2, a3, c], q3_s.at[p, 1], q3_r.at[p, rel, 1], sib)
            urx[p][a2, a3, c] = utx[p][c, a3, a2]

    for rel in (2, 1, 3, 0):
        for p in range(3):
            a2 = coordinate(p, 1, rel)
            arrived(urx[p].at[a2, few], q3_s.at[p, 0], q3_r.at[p, rel, 0])
            arrived(urx[p].at[a2, 0, 0], q3_s.at[p, 1], q3_r.at[p, rel, 1])
            sums = lax.dot_general(
                sel[p, rel], urx[p][a2].reshape(128, CW[p]), (((0,), (0,)), ((), ())), preferred_element_type=F32
            )
            if rel:
                ltx[p][rel - 1] = sums.astype(BF16).reshape(4, 16, CW[p])
                send(ltx[p].at[rel - 1], lrx[p].at[rel - 1], q2_s.at[p], q2_r.at[p], near(p, 1, rel))
            else:
                line[p][...] = sums.reshape(4, 16, CW[p])
    for p in range(3):
        total = line[p][...]
        arrived(lrx[p], q2_s.at[p], q2_r.at[p])
        for k in range(3):
            total = total + lrx[p][k].astype(F32)
        line[p][...] = total
        btx[p][...] = total.astype(BF16)
        for k, d in enumerate(STEPS):
            send(btx[p].at[coordinate(p, 0, d)], brx[p].at[k], q1_s.at[p], q1_r.at[p], near(p, 0, d))
    pieces = []
    for p in range(3):
        total = line[p][coordinate(p, 0, 0)]
        arrived(brx[p], q1_s.at[p], q1_r.at[p])
        for k in range(3):
            total = total + brx[p][k].astype(F32)
        pieces.append(total)
    mixed = (kept[...] + jnp.concatenate(pieces, axis=1)).astype(BF16).astype(F32)
    fin_tx[...] = jnp.where(first, mixed[8:], mixed[:8])
    send(fin_tx, fin_rx, pair_s.at[4], pair_r.at[4], sib)
    out[:, own_cols] = jnp.where(first, mixed[:8], mixed[8:]).astype(BF16)
    arrived(fin_rx, pair_s.at[4], pair_r.at[4])
    out[:, other_cols] = fin_rx[...].astype(BF16)

    for i, view in ((0, res_tx), (2, sq_tx), (3, table.at[:, :, :, c]), (4, fin_tx)):
        sent(view, pair_s.at[i])
    sent(att.at[pl.ds(1, 7)], a2a_s.at[0])
    sent(att_rx.at[:, c], af_s.at[0])
    sent(y_tx.at[pl.ds(1, 7)], y_s.at[0])
    sent(table.at[few, y, z, c], sh_s.at[0])
    sent(table.at[:, few, z, c], sh_s.at[1])
    sent(table.at[:, :, few, c], sh_s.at[2])
    for p in range(3):
        sent(at(p, few, 0), g1_s.at[p])
        sent(at(p, few, slice(None)), g2_s.at[p])
        sent(stx[p].at[:, few], g3_s.at[p, 0])
        sent(stx[p].at[:, 0, 0], g3_s.at[p, 1])
        sent(utx[p].at[:, few], q3_s.at[p, 0])
        sent(utx[p].at[0, 0], q3_s.at[p, 1])
        sent(ltx[p], q2_s.at[p])
        sent(btx[p].at[few], q1_s.at[p])


def local(
    residual, queries, key_cache, value_cache, new_keys, new_values, lengths, out_weight, norm_gain,
    routes, gate_probs, w_gate, w_up, w_down,
):
    vm = pl.BlockSpec(memory_space=pltpu.VMEM)
    hbm = pl.BlockSpec(memory_space=pl.ANY)
    dma = pltpu.SemaphoreType.DMA

    def v(*shape, dtype=BF16):
        return pltpu.VMEM(shape, dtype)

    scratch = [
        v(ROWS, D), v(ROWS, HQ * HD), v(ROWS, KVH * HD), v(ROWS, KVH * HD), pltpu.SMEM((ROWS,), jnp.int32),
        v(1, D, dtype=F32), v(ROWS, TOP, dtype=jnp.int32), v(ROWS, TOP, dtype=F32),
        v(ROWS, CACHE, KVH * HD), v(ROWS, CACHE, KVH * HD), v(1024, HALF), v(D, 2 * EH), v(EH, D),
        v(8, 64, HD), v(8, 2, 64, HD), v(128, 1024), v(8, 16, HALF), v(8, 16, HALF),
        v(8, HALF, dtype=F32), v(8, HALF, dtype=F32), v(16, 128, dtype=F32), v(16, 128, dtype=F32),
        v(4, 4, 4, 2, 8, 128, dtype=F32),
        *[v(4, 4, 16, w) for w in CW],
        v(3, 4, 128, 64), v(2, 256, 256), v(2, 256, 256), v(16, 16, 128, dtype=F32),
        *[v(4, 4, 2, 16, w) for w in CW],
        *[v(2, 4, 4, 16, w) for w in CW],
        v(256, 2 * EH, dtype=F32), v(3, 256, EH),
        *[v(2, 4, 4, 16, w) for w in CW],
        *[v(4, 4, 2, 16, w) for w in CW],
        *[v(3, 4, 16, w) for w in CW],
        *[v(3, 4, 16, w) for w in CW],
        *[v(4, 16, w, dtype=F32) for w in CW],
        *[v(4, 16, w) for w in CW],
        *[v(3, 16, w) for w in CW],
        v(16, HALF, dtype=F32), v(8, HALF, dtype=F32), v(8, HALF, dtype=F32),
        dma((7,)), dma((8,)), dma((5,)), dma((5,)), dma((1,)), dma((8,)), dma((1,)), dma((1,)), dma((1,)), dma((1,)),
        dma((3,)), dma((3,)), dma((3,)), dma((3, 3)), dma((3,)), dma((3, 3)),
        dma((3, 2)), dma((3, 2)), dma((3, 2)), dma((3, 4, 2)), dma((3,)), dma((3,)), dma((3,)), dma((3,)),
    ]
    return pl.pallas_call(
        kernel,
        out_shape=jax.ShapeDtypeStruct((ROWS, D), BF16),
        in_specs=[hbm] * 14,
        out_specs=vm,
        scratch_shapes=scratch,
        compiler_params=pltpu.CompilerParams(
            collective_id=0, has_side_effects=True, vmem_limit_bytes=58 * 2**20
        ),
        cost_estimate=pl.CostEstimate(flops=12 * 10**9, bytes_accessed=24 * 2**20, transcendentals=10**6),
    )(
        residual, queries, key_cache, value_cache, new_keys, new_values, lengths, out_weight,
        norm_gain.reshape(1, D), routes, gate_probs, w_gate, w_up, w_down,
    )


def solution(mesh):
    both = ("wide", "narrow")
    rows, cubes = P(both, None), P(both, None, None)
    in_specs = (
        rows, rows, cubes, cubes, rows, rows, P(both), P("narrow", None), P(), rows, rows, cubes, cubes, cubes,
    )
    return jax.shard_map(local, mesh=mesh, in_specs=in_specs, out_specs=rows, check_vma=False)
```

```python
import functools

import jax
import jax.numpy as jnp
from jax import lax
from jax.experimental import pallas as pl
from jax.experimental.pallas import tpu as pltpu
from jax.sharding import PartitionSpec as P

MESH = pl.DeviceIdType.MESH
F32 = jnp.float32
BF16 = jnp.bfloat16

D = 4096
HALF = 2048
HQ = 64
KVH = 4
HD = 128
TOP = 8
CACHE = 256
ROWS = 8
EH = 384

CW = (640, 640, 768)
OFF = (0, 640, 1280)
ORD = ((0, 1, 2), (1, 2, 0), (2, 0, 1))
STEPS = (1, 3, 2)


def coords():
    w, n = lax.axis_index("wide"), lax.axis_index("narrow")
    c = lax.rem(w, 2)
    z = lax.rem(lax.div(w, 2), 4)
    x = lax.div(n, 4) * 2 + lax.div(w, 8)
    return (x, lax.rem(n, 4), z), c, w * 8 + n, n


def device(pos, c):
    x, y, z = pos
    return (lax.rem(x, 2) * 8 + z * 2 + c, lax.div(x, 2) * 4 + y)


def shift(pos, axis, d):
    moved = list(pos)
    moved[axis] = lax.rem(moved[axis] + d, 4)
    return tuple(moved)


def remote(src, dst, ssem, rsem, target):
    return pltpu.make_async_remote_copy(
        src_ref=src, dst_ref=dst, send_sem=ssem, recv_sem=rsem, device_id=target, device_id_type=MESH
    )


def slab_index(p, first=slice(None), second=slice(None)):
    order = ORD[p]
    spec = {order[0]: first, order[1]: second}
    return tuple(spec[axis] for axis in range(3) if axis != order[2])


def kernel(
    residual_in, queries_in, key_cache, value_cache, new_keys_in, new_values_in, lengths_in, out_weight, gain_in,
    routes_in, probs_in, w_gate, w_up, w_down,
    out,
    residual, queries, new_keys, new_values, lengths, norm_gain, routes, gate_probs,
    keys, values, wo, wgu, wd, att, att_rx, a_mat, y_tx, y_rx, res_tx, res_rx, sq_tx, sq_rx,
    table, plane0, plane1, plane2, sel, perm, unperm, weight, stx0, stx1, stx2, srx0, srx1, srx2, acc, act,
    utx0, utx1, utx2, urx0, urx1, urx2, ltx0, ltx1, ltx2, lrx0, lrx1, lrx2, line0, line1, line2,
    btx0, btx1, btx2, brx0, brx1, brx2, kept, fin_tx, fin_rx,
    lsem, small, pair_s, pair_r, a2a_s, a2a_r, af_s, af_r, y_s, y_r, sh_s, sh_r,
    g1_s, g1_r, g2_s, g2_r, g3_s, g3_r, q3_s, q3_r, q2_s, q2_r, q1_s, q1_r,
):
    pos, c, me, n_me = coords()
    x, y, z = pos
    sib = device(pos, 1 - c)
    plane = (plane0, plane1, plane2)
    stx, srx, utx, urx = (stx0, stx1, stx2), (srx0, srx1, srx2), (utx0, utx1, utx2), (urx0, urx1, urx2)
    ltx, lrx, line = (ltx0, ltx1, ltx2), (lrx0, lrx1, lrx2), (line0, line1, line2)
    btx, brx = (btx0, btx1, btx2), (brx0, brx1, brx2)
    own_cols = pl.ds(pl.multiple_of(c * HALF, HALF), HALF)
    other_cols = pl.ds(pl.multiple_of((1 - c) * HALF, HALF), HALF)
    few = pl.ds(0, 3)

    def send(src, dst, ssem, rsem, target):
        remote(src, dst, ssem, rsem, target).start()

    def sent(src, ssem):
        remote(src, src, ssem, ssem, sib).wait_send()

    def arrived(dst, ssem, rsem):
        remote(dst, dst, ssem, rsem, sib).wait_recv()

    group = [(dx, dy) for dx in range(2) for dy in range(4)]

    def member(dx, dy):
        gx = x if dx == 0 else 3 - x
        gy = lax.rem(y + dy, 4)
        return (gx, gy, z), lax.div(gx, 2) * 4 + gy

    local = [
        pltpu.make_async_copy(key_cache, keys, lsem.at[0]),
        pltpu.make_async_copy(value_cache, values, lsem.at[1]),
        pltpu.make_async_copy(out_weight.at[:, own_cols], wo, lsem.at[2]),
        pltpu.make_async_copy(w_gate.at[0], wgu.at[:, pl.ds(0, EH)], lsem.at[3]),
        pltpu.make_async_copy(w_up.at[0], wgu.at[:, pl.ds(EH, EH)], lsem.at[4]),
        pltpu.make_async_copy(w_down.at[0], wd, lsem.at[5]),
    ]
    arguments = [
        pltpu.make_async_copy(src, dst, small.at[i])
        for i, (src, dst) in enumerate((
            (lengths_in, lengths), (queries_in, queries), (new_keys_in, new_keys), (new_values_in, new_values),
            (routes_in, routes), (probs_in, gate_probs), (residual_in, residual), (gain_in, norm_gain),
        ))
    ]
    for copy in arguments:
        copy.start()
    for copy in local[:3]:
        copy.start()

    barrier = pltpu.get_barrier_semaphore()
    partners = [sib] + [device(shift(pos, a, d), c) for a in range(3) for d in STEPS]
    partners += [device(shift(pos, a, d), 1 - c) for a in range(3) for d in STEPS]
    partners += [device(member(1, dy)[0], c) for dy in (1, 2, 3)]
    for partner in partners:
        pl.semaphore_signal(barrier, inc=1, device_id=partner, device_id_type=MESH)


    local[0].wait()
    local[1].wait()
    for copy in local[3:]:
        copy.start()
    for copy in arguments[:4]:
        copy.wait()
    scaling = HD ** (-0.5)
    row_request = lax.rem(lax.broadcasted_iota(jnp.int32, (128, CACHE), 0), ROWS)
    limit = jnp.zeros((128, CACHE), jnp.int32)
    for r in range(ROWS):
        limit = jnp.where(row_request == r, lengths[r], limit)
    visible = lax.broadcasted_iota(jnp.int32, (128, CACHE), 1) < limit
    def send_heads(n):
        same_side = lax.div(x, 2) == n // 4
        target = device((jnp.where(same_side, x, 3 - x), n % 4, z), c)

        @pl.when(n_me != n)
        def _():
            send(att.at[n], att_rx.at[n_me, c], a2a_s.at[0], a2a_r.at[n_me], target)

    for g in range(KVH):
        cols = slice(g * HD, (g + 1) * HD)
        q = jnp.concatenate(
            [queries[:, (g * 16 + h) * HD : (g * 16 + h + 1) * HD].astype(F32) for h in range(16)], axis=0
        )
        scores = lax.dot_general(
            q.astype(BF16), keys[:, :, cols].reshape(ROWS * CACHE, HD), (((1,), (1,)), ((), ())),
            preferred_element_type=F32,
        )
        picked = scores[:, :CACHE]
        for r in range(1, ROWS):
            picked = jnp.where(row_request == r, scores[:, r * CACHE : (r + 1) * CACHE], picked)
        picked = jnp.where(visible, picked * scaling, -jnp.inf)
        fresh = jnp.concatenate([new_keys[:, cols].astype(F32)] * 16, axis=0)
        own = jnp.sum(q * fresh, axis=-1, keepdims=True) * scaling
        highest = jnp.maximum(jnp.max(picked, axis=-1, keepdims=True), own)
        weights = jnp.exp(picked - highest)
        own = jnp.exp(own - highest)
        norm = jnp.sum(weights, axis=-1, keepdims=True) + own
        weights = weights / norm
        own = (own / norm).astype(BF16).astype(F32)
        spread = jnp.concatenate(
            [jnp.where(row_request == r, weights, 0.0).astype(BF16) for r in range(ROWS)], axis=1
        )
        got = jnp.dot(spread, values[:, :, cols].reshape(ROWS * CACHE, HD), preferred_element_type=F32)
        got = got + own * jnp.concatenate([new_values[:, cols].astype(F32)] * 16, axis=0)
        att[2 * g : 2 * g + 2] = got.astype(BF16).reshape(2, 64, HD)
        if g == 2:
            pl.semaphore_wait(barrier, len(partners))
            for n in range(6):
                send_heads(n)
    for n in (6, 7):
        send_heads(n)

    mine = pltpu.make_async_copy(att.at[n_me], att_rx.at[n_me, c], lsem.at[6])
    mine.start()
    for copy in arguments[4:]:
        copy.wait()
    probs = gate_probs[...]
    shares = probs / jnp.sum(probs, axis=-1, keepdims=True)
    lanes = lax.broadcasted_iota(jnp.int32, (ROWS, 128), 1)
    dense = jnp.zeros((ROWS, 128), F32)
    named = jnp.zeros((ROWS, 128), F32)
    chosen = routes[...]
    for k in range(TOP):
        hit = chosen[:, k : k + 1] == lanes
        dense = dense + jnp.where(hit, shares[:, k : k + 1], 0.0)
        named = named + jnp.where(hit, 1.0, 0.0)
    earlier, running = [], jnp.zeros((1, 128), F32)
    for t in range(ROWS):
        earlier.append(running)
        running = running + named[t : t + 1]
    earlier = jnp.concatenate(earlier, axis=0)
    number = lax.broadcasted_iota(jnp.int32, (ROWS, 128), 0).astype(F32) + 1.0
    entries = []
    for value in (number, dense):
        for r in range(2):
            taken = jnp.where(earlier == float(r), named * value, 0.0)
            entries.append(jnp.sum(taken, axis=0, keepdims=True) - (1.0 if value is number else 0.0))
    table[x, y, z, c] = jnp.concatenate(entries + [jnp.zeros((4, 128), F32)], axis=0)
    res_tx[...] = residual[:, other_cols].astype(F32)
    send(res_tx, res_rx, pair_s.at[0], pair_r.at[0], sib)
    for d in STEPS:
        view = table.at[x, y, z, c]
        send(view, view, sh_s.at[0], sh_r.at[0], device(shift(pos, 0, d), c))
    mine.wait()
    for i, (dx, dy) in enumerate(group):
        _, n = member(dx, (4 - dy) % 4)
        view = att_rx.at[n, c]
        if i:
            arrived(view, a2a_s.at[0], a2a_r.at[n])
        send(view, view, af_s.at[0], af_r.at[0], sib)
    arrived(att_rx.at[:, 1 - c], af_s.at[0], af_r.at[0])

    arrived(table.at[few, y, z, c], sh_s.at[0], sh_r.at[0])
    for d in STEPS:
        view = table.at[:, y, z, c]
        send(view, view, sh_s.at[1], sh_r.at[1], device(shift(pos, 1, d), c))
    heads = att_rx[...].astype(F32).reshape(16, 64, HD)
    for h in range(8):
        a_mat[:, h * HD : (h + 1) * HD] = heads[:, h * 8 : (h + 1) * 8].reshape(128, HD).astype(BF16)

    local[2].wait()
    for j in range(4):
        cols = pl.ds(j * 512, 512)
        sums = jnp.dot(a_mat[...], wo[:, cols], preferred_element_type=F32)
        y_tx[:, :, cols] = sums.astype(BF16).reshape(8, 16, 512)
        for i, (dx, dy) in enumerate(group):
            if i:
                target, n = member(dx, dy)
                send(y_tx.at[n, :, cols], y_rx.at[i, :, cols], y_s.at[0], y_r.at[0], device(target, c))
    arrived(table.at[:, few, z, c], sh_s.at[1], sh_r.at[1])
    for d in STEPS:
        view = table.at[:, :, z, c]
        send(view, view, sh_s.at[2], sh_r.at[2], device(shift(pos, 2, d), c))

    big_r = lax.broadcasted_iota(jnp.int32, (256, 256), 0)
    big_c = lax.broadcasted_iota(jnp.int32, (256, 256), 1)

    def common(i, p):
        digits = {ORD[p][2]: lax.div(i, 64), ORD[p][1]: lax.rem(lax.div(i, 16), 4), ORD[p][0]: lax.rem(lax.div(i, 4), 4)}
        return digits[2] * 64 + digits[1] * 16 + digits[0] * 4 + lax.rem(i, 4)

    for p in (1, 2):
        perm[p - 1] = jnp.where(big_r == common(big_c, p), 1.0, 0.0).astype(BF16)
        unperm[p - 1] = jnp.where(common(big_r, p) == big_c, 1.0, 0.0).astype(BF16)
    arrived(res_rx, pair_s.at[0], pair_r.at[0])
    own_res, other_res = residual[:, own_cols].astype(F32), res_rx[...]
    first = c == 0
    total = jnp.concatenate(
        [jnp.where(first, own_res, other_res), jnp.where(first, other_res, own_res)], axis=0
    )
    attention = y_tx[n_me].astype(F32)
    arrived(y_rx.at[pl.ds(1, 7)], y_s.at[0], y_r.at[0])
    for i in range(1, 8):
        attention = attention + y_rx[i].astype(F32)
    arrived(table.at[:, :, few, c], sh_s.at[2], sh_r.at[2])
    view = table.at[:, :, :, c]
    send(view, view, pair_s.at[3], pair_r.at[3], sib)
    stream = (total + attention).astype(BF16).astype(F32)
    squares = jnp.sum(stream * stream, axis=-1, keepdims=True)
    sq_tx[...] = jnp.broadcast_to(squares, (16, 128))
    send(sq_tx, sq_rx, pair_s.at[2], pair_r.at[2], sib)
    kept[...] = stream
    arrived(sq_rx, pair_s.at[2], pair_r.at[2])
    mean = (squares + sq_rx[:, 0:1]) * (1.0 / D)
    normed = (stream * lax.rsqrt(mean + 1e-06) * norm_gain[:, own_cols]).astype(BF16)
    for p in range(3):
        plane[p][slab_index(p, pos[ORD[p][0]], pos[ORD[p][1]])] = normed[:, OFF[p] : OFF[p] + CW[p]]

    def at(p, first, second):
        return plane[p].at[slab_index(p, first, second)]

    def near(p, stage, d, core=c):
        return device(shift(pos, ORD[p][stage], d), core)

    def coordinate(p, stage, d):
        return lax.rem(pos[ORD[p][stage]] + d, 4)

    def along(p, i, d):
        return coordinate(p, 0, 0 if i == 0 else 4 - STEPS[i - 1]), coordinate(p, 1, d)

    def spread_block(p, i):
        view = at(p, *along(p, i, 0))
        for k, d in enumerate(STEPS):
            send(view, view, g2_s.at[p], g2_r.at[p, k], near(p, 1, d))

    for p in range(3):
        view = at(p, *along(p, 0, 0))
        for k, d in enumerate(STEPS):
            send(view, view, g1_s.at[p], g1_r.at[p, k], near(p, 0, d))
    for p in range(3):
        spread_block(p, 0)

    arrived(table.at[:, :, :, 1 - c], pair_s.at[3], pair_r.at[3])
    slot = lax.broadcasted_iota(jnp.int32, (16, 64), 0)
    token = lax.broadcasted_iota(jnp.int32, (16, 64), 1)
    same = lax.div(slot, 2) == lax.div(token, 8)
    place = lax.rem(token, 8)
    take_token = jnp.where(same & (place == lax.rem(slot, 2)), 1.0, 0.0).astype(BF16)
    take_share = jnp.where(same & (place == lax.rem(slot, 2) + 2), 1.0, 0.0).astype(BF16)
    place = place.astype(F32)
    lane16 = lax.broadcasted_iota(jnp.int32, (16, 128), 1)

    def expert_of(where, core):
        ex, ey, ez = where
        return lax.div(((lax.rem(ex, 2) * 8 + ez * 2 + core) * 8) + lax.div(ex, 2) * 4 + ey, 2)

    for p in range(3):
        for rel in range(4):
            idx = list(pos)
            idx[ORD[p][0]], idx[ORD[p][1]] = slice(None), coordinate(p, 1, rel)
            entries = table[tuple(idx)].reshape(64, 128).astype(BF16)
            numbers = jnp.dot(take_token, entries, preferred_element_type=F32)
            for q in range(4):
                chip = list(pos)
                chip[ORD[p][2]] = q
                for core in range(2):
                    wanted = jnp.sum(
                        jnp.where(lane16 == expert_of(chip, core), numbers, 0.0), axis=-1, keepdims=True
                    )
                    hits = jnp.where(same & (wanted == place), 1.0, 0.0)
                    sel[p, rel, (q * 2 + core) * 16 : (q * 2 + core + 1) * 16] = hits.astype(BF16)

    def dispatch(p, rel):
        rows = plane[p][slab_index(p, slice(None), coordinate(p, 1, rel))].reshape(64, CW[p])
        picked = jnp.dot(sel[p, rel], rows, preferred_element_type=F32).astype(BF16)
        stx[p][rel] = picked.reshape(4, 2, 16, CW[p])
        a3, a2 = coordinate(p, 2, 0), coordinate(p, 1, rel)
        spot = srx[p].at[c, a3, a2]
        for dq in STEPS:
            for core in range(2):
                send(
                    stx[p].at[rel, coordinate(p, 2, dq), core], spot,
                    g3_s.at[p, 0], g3_r.at[p, 0], near(p, 2, dq, core),
                )
        send(stx[p].at[rel, a3, 1 - c], spot, g3_s.at[p, 1], g3_r.at[p, 1], sib)
        srx[p][c, a3, a2] = stx[p][rel, a3, c]

    for k, d in enumerate(STEPS):
        for p in range(3):
            arrived(at(p, *along(p, k + 1, 0)), g1_s.at[p], g1_r.at[p, k])
            spread_block(p, k + 1)
    for p in range(3):
        dispatch(p, 0)
    for k, d in enumerate(STEPS):
        for p in range(3):
            arrived(at(p, slice(None), coordinate(p, 1, 4 - d)), g2_s.at[p], g2_r.at[p, k])
            dispatch(p, 4 - d)

    mine_expert = lax.div(me, 2)

    @pl.loop(0, 16)
    def _(i):
        entries = table[:, lax.rem(i, 4), lax.div(i, 4)].reshape(64, 128)
        high = entries.astype(BF16)
        low = (entries - high.astype(F32)).astype(BF16)
        values = jnp.dot(take_share, high, preferred_element_type=F32)
        values = values + jnp.dot(take_share, low, preferred_element_type=F32)
        found = jnp.sum(jnp.where(lane16 == mine_expert, values, 0.0), axis=-1, keepdims=True)
        weight[i] = jnp.broadcast_to(found, (16, 128))

    for copy in local[3:]:
        copy.wait()

    for p in range(3):
        arrived(srx[p].at[:, few], g3_s.at[p, 0], g3_r.at[p, 0])
        arrived(srx[p].at[0, 0], g3_s.at[p, 1], g3_r.at[p, 1])
        for half in range(2):
            rows = srx[p][half].reshape(256, CW[p])
            if p:
                rows = jnp.dot(perm[p - 1], rows, preferred_element_type=F32).astype(BF16)
            k = slice(half * HALF + OFF[p], half * HALF + OFF[p] + CW[p])
            sums = jnp.dot(rows, wgu[k, :], preferred_element_type=F32)
            acc[...] = sums if p == 0 and half == 0 else acc[...] + sums
    gate, up = acc[:, :EH], acc[:, EH:]
    shares = weight[...].reshape(256, 128)[:, 0:1]
    active = (gate / (1.0 + jnp.exp(-gate)) * up * shares).astype(BF16)
    act[0] = active
    for p in (1, 2):
        act[p] = jnp.dot(unperm[p - 1], active, preferred_element_type=F32).astype(BF16)

    def give_back(p, half, rel):
        a3, a2 = coordinate(p, 2, 0), coordinate(p, 1, rel)
        spot = urx[p].at[a2, a3, c]
        for dq in STEPS:
            send(
                utx[p].at[half, coordinate(p, 2, dq), a2], spot,
                q3_s.at[p, 0], q3_r.at[p, rel, 0], near(p, 2, dq, half),
            )

    for half in range(2):
        for p in range(3):
            cols = slice(half * HALF + OFF[p], half * HALF + OFF[p] + CW[p])
            sums = jnp.dot(act[p], wd[:, cols], preferred_element_type=F32)
            utx[p][half] = sums.astype(BF16).reshape(4, 4, 16, CW[p])
            give_back(p, half, 2)
    for rel in (2, 1, 3, 0):
        for p in range(3):
            a3, a2 = coordinate(p, 2, 0), coordinate(p, 1, rel)
            if rel != 2:
                for half in range(2):
                    give_back(p, half, rel)
            send(utx[p].at[1 - c, a3, a2], urx[p].at[a2, a3, c], q3_s.at[p, 1], q3_r.at[p, rel, 1], sib)
            urx[p][a2, a3, c] = utx[p][c, a3, a2]

    for rel in (2, 1, 3, 0):
        for p in range(3):
            a2 = coordinate(p, 1, rel)
            arrived(urx[p].at[a2, few], q3_s.at[p, 0], q3_r.at[p, rel, 0])
            arrived(urx[p].at[a2, 0, 0], q3_s.at[p, 1], q3_r.at[p, rel, 1])
            sums = lax.dot_general(
                sel[p, rel], urx[p][a2].reshape(128, CW[p]), (((0,), (0,)), ((), ())), preferred_element_type=F32
            )
            if rel:
                ltx[p][rel - 1] = sums.astype(BF16).reshape(4, 16, CW[p])
                send(ltx[p].at[rel - 1], lrx[p].at[rel - 1], q2_s.at[p], q2_r.at[p], near(p, 1, rel))
            else:
                line[p][...] = sums.reshape(4, 16, CW[p])
    for p in range(3):
        total = line[p][...]
        arrived(lrx[p], q2_s.at[p], q2_r.at[p])
        for k in range(3):
            total = total + lrx[p][k].astype(F32)
        line[p][...] = total
        btx[p][...] = total.astype(BF16)
        for k, d in enumerate(STEPS):
            send(btx[p].at[coordinate(p, 0, d)], brx[p].at[k], q1_s.at[p], q1_r.at[p], near(p, 0, d))
    pieces = []
    for p in range(3):
        total = line[p][coordinate(p, 0, 0)]
        arrived(brx[p], q1_s.at[p], q1_r.at[p])
        for k in range(3):
            total = total + brx[p][k].astype(F32)
        pieces.append(total)
    mixed = (kept[...] + jnp.concatenate(pieces, axis=1)).astype(BF16).astype(F32)
    fin_tx[...] = jnp.where(first, mixed[8:], mixed[:8])
    send(fin_tx, fin_rx, pair_s.at[4], pair_r.at[4], sib)
    out[:, own_cols] = jnp.where(first, mixed[:8], mixed[8:]).astype(BF16)
    arrived(fin_rx, pair_s.at[4], pair_r.at[4])
    out[:, other_cols] = fin_rx[...].astype(BF16)

    for i, view in ((0, res_tx), (2, sq_tx), (3, table.at[:, :, :, c]), (4, fin_tx)):
        sent(view, pair_s.at[i])
    sent(att.at[pl.ds(1, 7)], a2a_s.at[0])
    sent(att_rx.at[:, c], af_s.at[0])
    sent(y_tx.at[pl.ds(1, 7)], y_s.at[0])
    sent(table.at[few, y, z, c], sh_s.at[0])
    sent(table.at[:, few, z, c], sh_s.at[1])
    sent(table.at[:, :, few, c], sh_s.at[2])
    for p in range(3):
        sent(at(p, few, 0), g1_s.at[p])
        sent(at(p, few, slice(None)), g2_s.at[p])
        sent(stx[p].at[:, few], g3_s.at[p, 0])
        sent(stx[p].at[:, 0, 0], g3_s.at[p, 1])
        sent(utx[p].at[:, few], q3_s.at[p, 0])
        sent(utx[p].at[0, 0], q3_s.at[p, 1])
        sent(ltx[p], q2_s.at[p])
        sent(btx[p].at[few], q1_s.at[p])


def local(
    residual, queries, key_cache, value_cache, new_keys, new_values, lengths, out_weight, norm_gain,
    routes, gate_probs, w_gate, w_up, w_down,
):
    vm = pl.BlockSpec(memory_space=pltpu.VMEM)
    hbm = pl.BlockSpec(memory_space=pl.ANY)
    dma = pltpu.SemaphoreType.DMA

    def v(*shape, dtype=BF16):
        return pltpu.VMEM(shape, dtype)

    scratch = [
        v(ROWS, D), v(ROWS, HQ * HD), v(ROWS, KVH * HD), v(ROWS, KVH * HD), pltpu.SMEM((ROWS,), jnp.int32),
        v(1, D, dtype=F32), v(ROWS, TOP, dtype=jnp.int32), v(ROWS, TOP, dtype=F32),
        v(ROWS, CACHE, KVH * HD), v(ROWS, CACHE, KVH * HD), v(1024, HALF), v(D, 2 * EH), v(EH, D),
        v(8, 64, HD), v(8, 2, 64, HD), v(128, 1024), v(8, 16, HALF), v(8, 16, HALF),
        v(8, HALF, dtype=F32), v(8, HALF, dtype=F32), v(16, 128, dtype=F32), v(16, 128, dtype=F32),
        v(4, 4, 4, 2, 8, 128, dtype=F32),
        *[v(4, 4, 16, w) for w in CW],
        v(3, 4, 128, 64), v(2, 256, 256), v(2, 256, 256), v(16, 16, 128, dtype=F32),
        *[v(4, 4, 2, 16, w) for w in CW],
        *[v(2, 4, 4, 16, w) for w in CW],
        v(256, 2 * EH, dtype=F32), v(3, 256, EH),
        *[v(2, 4, 4, 16, w) for w in CW],
        *[v(4, 4, 2, 16, w) for w in CW],
        *[v(3, 4, 16, w) for w in CW],
        *[v(3, 4, 16, w) for w in CW],
        *[v(4, 16, w, dtype=F32) for w in CW],
        *[v(4, 16, w) for w in CW],
        *[v(3, 16, w) for w in CW],
        v(16, HALF, dtype=F32), v(8, HALF, dtype=F32), v(8, HALF, dtype=F32),
        dma((7,)), dma((8,)), dma((5,)), dma((5,)), dma((1,)), dma((8,)), dma((1,)), dma((1,)), dma((1,)), dma((1,)),
        dma((3,)), dma((3,)), dma((3,)), dma((3, 3)), dma((3,)), dma((3, 3)),
        dma((3, 2)), dma((3, 2)), dma((3, 2)), dma((3, 4, 2)), dma((3,)), dma((3,)), dma((3,)), dma((3,)),
    ]
    return pl.pallas_call(
        kernel,
        out_shape=jax.ShapeDtypeStruct((ROWS, D), BF16),
        in_specs=[hbm] * 14,
        out_specs=vm,
        scratch_shapes=scratch,
        compiler_params=pltpu.CompilerParams(
            collective_id=0, has_side_effects=True, vmem_limit_bytes=58 * 2**20
        ),
        cost_estimate=pl.CostEstimate(flops=12 * 10**9, bytes_accessed=24 * 2**20, transcendentals=10**6),
    )(
        residual, queries, key_cache, value_cache, new_keys, new_values, lengths, out_weight,
        norm_gain.reshape(1, D), routes, gate_probs, w_gate, w_up, w_down,
    )


def solution(mesh):
    both = ("wide", "narrow")
    rows, cubes = P(both, None), P(both, None, None)
    in_specs = (
        rows, rows, cubes, cubes, rows, rows, P(both), P("narrow", None), P(), rows, rows, cubes, cubes, cubes,
    )
    return jax.shard_map(local, mesh=mesh, in_specs=in_specs, out_specs=rows, check_vma=False)
```
